32 devices in a mesh: groups: 2 (over x), dp: 16 (over z, y, core).
Axes of the slice: x: 2, y: 2, z: 4, core: 2. Of those that a mesh axis runs over, the one named last changes fastest.
Arguments:
- train_grads: bfloat16 [32768, 1024], P(('groups', 'dp')), parts along dimension 0, as said below
- eval_grads: bfloat16 [2048, 1024], P(('groups', 'dp')), parts along dimension 0, may hold values from -6 to 6
- pair_eval: int32 [32, 4], P('groups'), parts along dimension 0, may hold values from 0 to 3, each once within a row
- pair_count: int32 [32], P('groups'), parts along dimension 0, may hold values from 1 to 4, as said below
Outputs:
- influence: float32 [4, 32768], P(None, ('groups', 'dp')), parts along dimension 1
The draws below stay inside these ranges and needn't reach their ends.
There are 2 independent parts, one for each index of `groups`. The reference program is written for one: setup_inputs(seed, part) draws one part's arguments, and reference() takes and returns one part's arrays. A program takes and returns all parts, laid end to end along the dimension named above; each array names one. Nothing has to cross between parts.
Inputs may be any that keep to these rules, and one draw needn't show every extreme that they name: `train_grads`: entries are real-valued gradients of varying scale. `pair_count`: the largest count equals 4 in every draw.
All inputs are finite; a program needn't handle non-finite values.
Results may differ from the reference program's by a relative error of at most 0.0015.
Values may be sent and summed in bfloat16 or wider, within the bound.
No kernel may reach another device: no remote copies, remote signals or barrier semaphores. Data moves between devices by JAX's collectives and lax.ppermute only.
A program may use at most 64 MiB of HBM per device.

```python
import math
import jax
import jax.numpy as jnp
from jax import lax

K = 1024
TR_DEV = 1024
EB = 256
NTB = 16
NTRAIN = 16384
NEV = 1024
NEB = 4


def draw_train_grads(key, part):
    key = jax.random.fold_in(key, 11)
    key_row, key_col, key_entry = jax.random.split(key, 3)
    place = jnp.arange(NTRAIN, dtype=jnp.float32)[:, None] / NTRAIN
    entries = jax.random.normal(key_entry, (NTRAIN, K), jnp.float32)
    spread = math.log(10.0)
    row_scale = jnp.exp(jax.random.uniform(key_row, (NTRAIN, 1), jnp.float32) * spread + math.log(3.0) * place)
    col_scale = jnp.exp(jax.random.uniform(key_col, (1, K), jnp.float32) * math.log(10.0))
    return (0.1 * entries * row_scale * col_scale).astype(jnp.bfloat16)


def draw_pair_count(key, part):
    key = jax.random.fold_in(key, 23)
    key_base, key_domain, key_hot, key_pick = jax.random.split(key, 4)
    base = jax.random.randint(key_base, (NTB,), max(NEB // 8, 1), max(NEB // 4, 1) + 1)
    domain = jax.random.randint(key_domain, (NTB,), 0, 8)
    hot = jax.random.randint(key_hot, (), 0, 8)
    pick = jax.random.randint(key_pick, (), 0, NTB)
    domain = jnp.where(jnp.arange(NTB) == pick, hot, domain)
    return jnp.where(domain == hot, NEB, base).astype(jnp.int32)


def shard_levels(rng, extent, shards, low, largest):
    level, own = 1.0, jax.random.fold_in(rng, 6)
    for position, parts in shards:
        heights = jnp.exp(jax.random.uniform(jax.random.fold_in(own, position), (parts,), jnp.float32, low / len(shards), largest / len(shards)))
        level = level * jnp.repeat(heights, extent[position] // parts).reshape([-1 if axis == position else 1 for axis in range(len(extent))])
    return level


def centred(stream_key, shape, width, most, cuts=(), kind=jnp.bfloat16):
    gain = shard_levels(stream_key, shape, cuts, -0.22, 0.18) if cuts else 1.0
    values = jax.random.normal(stream_key, shape, jnp.float32) * width * gain
    return jnp.minimum(jnp.maximum(values, -most), most).astype(kind)


def setup_inputs(seed: int = 0, part: int = 0) -> dict:
    keys = jax.random.split(jax.random.key(seed), 5)
    own_keys = jax.random.split(jax.random.fold_in(keys[4], part), 5)
    train_grads = draw_train_grads(jax.random.fold_in(jax.random.fold_in(keys[4], part), 71), part)
    eval_grads = centred(own_keys[1], (NEV, K), 1.0, 6.0, ((0, 16),))
    pair_eval = jax.vmap(lambda own: jax.random.permutation(own, NEB))(jax.random.split(own_keys[2], NTB)).reshape((NTB, NEB)).astype(jnp.int32)
    pair_count = draw_pair_count(jax.random.fold_in(jax.random.fold_in(keys[4], part), 71), part)
    return {"train_grads": train_grads, "eval_grads": eval_grads, "pair_eval": pair_eval, "pair_count": pair_count}


DAMPING = 0.1
EPSILON = 1e-06

def membership(pair_eval, pair_count):
    blocks = jnp.arange(NEB, dtype=jnp.int32)
    hits = pair_eval[:, :, None] == blocks[None, None, :]
    inside = blocks[None, :, None] < pair_count[:, None, None]
    return jnp.any(hits & inside, axis=1).astype(jnp.int32)

def reference(train_grads, eval_grads, pair_eval, pair_count):
    summed = lax.dot_general(train_grads.astype(jnp.float32), train_grads.astype(jnp.float32), (((0,), (0,)), ((), ())), preferred_element_type=jnp.float32)
    trace = jnp.trace(summed)
    gram = summed * (K / trace) + DAMPING * jnp.eye(K, dtype=jnp.float32)
    factor = jnp.linalg.cholesky(gram)
    half = lax.linalg.triangular_solve(factor, eval_grads.astype(jnp.float32), left_side=False, lower=True, transpose_a=True)
    precond = lax.linalg.triangular_solve(factor, half, left_side=False, lower=True).astype(jnp.bfloat16)
    inv_norm = lax.rsqrt(lax.optimization_barrier(jnp.sum(jnp.square(train_grads.astype(jnp.float32)), axis=1)) + EPSILON)
    listed = membership(pair_eval, pair_count)
    blocks = train_grads.reshape(NTB, TR_DEV, K)
    scales = inv_norm.reshape(NTB, TR_DEV)
    evals = precond.reshape(NEB, EB, K)

    def score_block(items):
        block, scale, flags = items

        def per_eval(eval_block):
            score = lax.dot_general(block.astype(jnp.float32), eval_block.astype(jnp.float32), (((1,), (1,)), ((), ())), preferred_element_type=jnp.float32)
            return lax.optimization_barrier(jnp.max(score, axis=1)) * scale
        tops = lax.map(per_eval, evals)
        return jnp.where(flags[:, None] > 0, tops, jnp.zeros_like(tops))
    result = lax.map(score_block, (blocks, scales, listed))
    return jnp.transpose(result, (1, 0, 2)).reshape(NEB, NTRAIN)
```

```python
import functools

import jax
import jax.numpy as jnp
from jax import lax
from jax.experimental import pallas as pl
from jax.experimental.pallas import tpu as pltpu
from jax.sharding import PartitionSpec as P

EB = 256
DAMPING = 0.1
EPSILON = 1e-06
B = 128
F32, BF16 = jnp.float32, jnp.bfloat16
NT = (((1,), (1,)), ((), ()))
NN = (((1,), (0,)), ((), ()))
TN = (((0,), (0,)), ((), ()))
VMEM_BYTES = 56 * 1024 * 1024


def dot(a, b, dims):
    return lax.dot_general(a, b, dims, preferred_element_type=F32)


def slab_offset(j, nb):
    return B * (j * nb - j * (j - 1) // 2)


def split3(x):
    hi = x.astype(BF16)
    rest = x - hi.astype(F32)
    mid = rest.astype(BF16)
    lo = (rest - mid.astype(F32)).astype(BF16)
    return hi, mid, lo


def left_parts(x):
    h, m, l = split3(x)
    return jnp.concatenate([h, h, m, m, h, l], axis=1)


def right_parts(x, axis=1):
    h, m, l = split3(x)
    return jnp.concatenate([h, m, h, m, l, h], axis=axis)


def gram_kernel(me_ref, t_ref, out_ref, packed, *, nb, pieces):
    width = nb * B
    for J in range(nb // 2):
        c0 = 2 * B * J
        g = dot(t_ref[:, c0:], t_ref[:, c0 : c0 + 2 * B], TN)
        o0, o1 = slab_offset(2 * J, nb), slab_offset(2 * J + 1, nb)
        packed[o0 : o0 + width - c0, :] = g[:, :B]
        packed[o1 : o1 + width - c0 - B, :] = g[B:, B:]
    rows = packed.shape[0] // pieces
    me = me_ref[0]
    for r in range(pieces):
        to = pl.multiple_of((me ^ r) * rows, 8)
        out_ref[pl.ds(to, rows), :] = packed[r * rows : (r + 1) * rows, :]


def local_gram(me, t, pieces):
    nb = t.shape[1] // B
    total = slab_offset(nb, nb)
    return pl.pallas_call(
        functools.partial(gram_kernel, nb=nb, pieces=pieces),
        out_shape=jax.ShapeDtypeStruct((total, B), F32),
        in_specs=[
            pl.BlockSpec(memory_space=pltpu.SMEM),
            pl.BlockSpec(memory_space=pltpu.VMEM),
        ],
        out_specs=pl.BlockSpec(memory_space=pltpu.VMEM),
        scratch_shapes=[pltpu.VMEM((total, B), F32)],
        compiler_params=pltpu.CompilerParams(vmem_limit_bytes=VMEM_BYTES),
        cost_estimate=pl.CostEstimate(
            flops=t.shape[0] * t.shape[1] * t.shape[1],
            bytes_accessed=t.size * 2 + total * B * 4,
            transcendentals=0,
        ),
        name="local_gram",
    )(me, t)


def invert_block(M):
    M = list(M)
    full = (8, B)
    lane = lax.broadcasted_iota(jnp.int32, full, 1)
    sub = lax.broadcasted_iota(jnp.int32, full, 0)
    n = len(M)
    for b in range(n):
        k0 = 8 * b
        R = [jnp.broadcast_to(M[b][i : i + 1, :], full) for i in range(8)]
        S = [
            [jnp.broadcast_to(R[i][:, k0 + j : k0 + j + 1], full) for j in range(i + 1)]
            for i in range(8)
        ]
        inside = (lane >= k0) & (lane < k0 + 8)
        R = [
            jnp.where(inside, jnp.where(lane == k0 + i, 1.0, 0.0).astype(F32), R[i])
            for i in range(8)
        ]
        m = [[None] * 8 for _ in range(8)]
        rc = [None] * 8
        for j in range(8):
            rc[j] = 1.0 / S[j][j]
            for i in range(j + 1, 8):
                m[i][j] = S[i][j] * rc[j]
            for i in range(j + 1, 8):
                for k in range(j + 1, i + 1):
                    S[i][k] = S[i][k] - m[i][j] * S[k][j]
            for i in range(j + 1, 8):
                R[i] = R[i] - m[i][j] * R[j]
        for i in range(7, -1, -1):
            R[i] = R[i] * rc[i]
            for j in range(i + 1, 8):
                R[i] = R[i] - m[j][i] * R[j]
        for q in range(1, n + 1):
            t = (b + q) % n
            if t == b:
                x = R[0]
                for i in range(1, 8):
                    x = jnp.where(sub == i, R[i], x)
            else:
                c = [jnp.broadcast_to(M[t][:, k0 + k : k0 + k + 1], full) for k in range(8)]
                x = jnp.where(inside, 0.0, M[t])
                for k in range(8):
                    x = x - c[k] * R[k]
            M[t] = x
    return M


def inverse_kernel(me_ref, g_ref, hi_ref, lo_ref, packed, A, D, WL, CR, *, nb, pieces):
    width = nb * B
    rows = packed.shape[0] // pieces
    me = me_ref[0]
    for r in range(pieces):
        at = pl.multiple_of((me ^ r) * rows, 8)
        packed[r * rows : (r + 1) * rows, :] = g_ref[pl.ds(at, rows), :]
    eye = lax.broadcasted_iota(jnp.int32, (B, B), 0) == lax.broadcasted_iota(
        jnp.int32, (B, B), 1
    )
    diag = jnp.zeros((B, B), F32)
    for j in range(nb):
        o = slab_offset(j, nb)
        diag = diag + jnp.where(eye, packed[o : o + B, :], 0.0)
    trace = jnp.sum(jnp.sum(diag, axis=1, keepdims=True), axis=0, keepdims=True)
    scale = jnp.broadcast_to(width / trace, (1, B))
    damp = jnp.where(eye, DAMPING, 0.0).astype(F32)
    for j in range(nb):
        o = slab_offset(j, nb)
        A[j, B * j : B * j + B, :] = packed[o : o + B, :] * scale + damp
        if j + 1 < nb:
            A[j, B * j + B :, :] = packed[o + B : o + width - B * j, :] * scale
    D[...] = A[0, :B, :]
    WL[...] = jnp.zeros_like(WL)
    CR[...] = jnp.zeros_like(CR)
    MC = 256

    def update():
        for J in range(nb // 2):
            right = CR[2 * B * J : 2 * B * (J + 1), :]
            for r in range(0, width, MC):
                u = dot(WL[r : r + MC, :], right, NT)
                A[2 * J, r : r + MC, :] = A[2 * J, r : r + MC, :] - u[:, :B]
                A[2 * J + 1, r : r + MC, :] = A[2 * J + 1, r : r + MC, :] - u[:, B:]

    def step(k, carry):
        inv = jnp.concatenate(invert_block([D[8 * t : 8 * t + 8, :] for t in range(B // 8)]))
        update()
        own = pl.ds(pl.multiple_of(k * B, B), B)
        A[k, own, :] = jnp.zeros((B, B), F32)
        C = A[k]
        CR[...] = right_parts(C)
        W = dot(left_parts(C), right_parts(inv, axis=0), NN)
        A[k] = W
        WL[...] = left_parts(W)
        A[k, own, :] = -inv
        WL[own, :] = left_parts(-inv)
        for j in range(nb):
            @pl.when(j != k)
            def _():
                A[j, own, :] = jnp.zeros((B, B), F32)

        @pl.when(k + 1 < nb)
        def _():
            nxt = pl.ds(pl.multiple_of((k + 1) * B, B), B)
            D[...] = A[k + 1, nxt, :] - dot(WL[nxt, :], CR[nxt, :], NT)

        return carry

    lax.fori_loop(0, nb, step, 0)
    update()
    for j in range(nb):
        x = -A[j]
        hi = x.astype(BF16)
        hi_ref[:, B * j : B * j + B] = hi
        lo_ref[:, B * j : B * j + B] = (x - hi.astype(F32)).astype(BF16)


def gram_inverse(me, g, nb, pieces):
    width = nb * B
    out = jax.ShapeDtypeStruct((width, width), BF16)
    return pl.pallas_call(
        functools.partial(inverse_kernel, nb=nb, pieces=pieces),
        out_shape=(out, out),
        in_specs=[
            pl.BlockSpec(memory_space=pltpu.SMEM),
            pl.BlockSpec(memory_space=pltpu.VMEM),
        ],
        out_specs=(pl.BlockSpec(memory_space=pltpu.VMEM),) * 2,
        scratch_shapes=[
            pltpu.VMEM(g.shape, F32),
            pltpu.VMEM((nb, width, B), F32),
            pltpu.VMEM((B, B), F32),
            pltpu.VMEM((width, 6 * B), BF16),
            pltpu.VMEM((width, 6 * B), BF16),
        ],
        compiler_params=pltpu.CompilerParams(vmem_limit_bytes=VMEM_BYTES),
        cost_estimate=pl.CostEstimate(
            flops=12 * width**3, bytes_accessed=g.size * 4 + width * width * 4, transcendentals=0
        ),
        name="gram_inverse",
    )(me, g)


def score_kernel(flag_ref, e_ref, hi_ref, lo_ref, t_ref, scale_ref, out_ref):
    e = pl.program_id(0)

    @pl.when(flag_ref[e] > 0)
    def _():
        rows = e_ref[...]
        pre = (dot(rows, hi_ref[...], NN) + dot(rows, lo_ref[...], NN)).astype(BF16)
        score = dot(pre, t_ref[...], NT)
        out_ref[pl.ds(e, 1), :] = jnp.max(score, axis=0, keepdims=True) * scale_ref[...]

    @pl.when(flag_ref[e] <= 0)
    def _():
        out_ref[pl.ds(e, 1), :] = jnp.zeros((1, out_ref.shape[1]), F32)


def scores(flags, evals, hi, lo, t, scale):
    blocks = evals.shape[0] // EB
    width = t.shape[1]
    whole = lambda shape: pl.BlockSpec(shape, lambda e: (0, 0))
    return pl.pallas_call(
        score_kernel,
        grid=(blocks,),
        out_shape=jax.ShapeDtypeStruct((blocks, t.shape[0]), F32),
        in_specs=[
            pl.BlockSpec(memory_space=pltpu.SMEM),
            pl.BlockSpec((EB, width), lambda e: (e, 0)),
            whole(hi.shape),
            whole(lo.shape),
            whole(t.shape),
            whole(scale.shape),
        ],
        out_specs=whole((blocks, t.shape[0])),
        compiler_params=pltpu.CompilerParams(vmem_limit_bytes=VMEM_BYTES),
        cost_estimate=pl.CostEstimate(
            flops=6 * evals.size * width,
            bytes_accessed=evals.size * 2 + width * width * 6,
            transcendentals=0,
        ),
        name="scores",
    )(flags, evals, hi, lo, t, scale)


def bit_groups(n):
    bits = [1 << s for s in range(n.bit_length() - 1)]
    groups = [[b] for b in bits[:2]]
    rest = bits[2:]
    while rest:
        groups.append(rest[:2])
        rest = rest[2:]
    return groups


def send(x, mask, n):
    return lax.ppermute(x, "dp", [(i, i ^ mask) for i in range(n)])


def place_of(index, n):
    place, step = 0, n
    for group in bit_groups(n):
        size = 1 << len(group)
        step //= size
        place = place + (index // group[0]) % size * step
    return place


def all_reduce(x, n):
    groups = bit_groups(n)
    for group in groups:
        size = 1 << len(group)
        part = x.shape[0] // size
        total = x[:part]
        for q in range(1, size):
            total = total + send(x[q * part : (q + 1) * part], q * group[0], n)
        x = total
    for group in reversed(groups):
        x = jnp.concatenate([x] + [send(x, q * group[0], n) for q in range(1, 1 << len(group))])
    return x


def per_device(train_grads, eval_grads, pair_eval, pair_count, n):
    width = train_grads.shape[1]
    nb = width // B
    index = lax.axis_index("dp")
    me = place_of(index, n)[None]
    packed = local_gram(me, train_grads, n)
    packed = all_reduce(packed, n)
    hi, lo = gram_inverse(me, packed, nb, n)
    evals = lax.all_gather(eval_grads, "dp", axis=0, tiled=True)
    blocks = evals.shape[0] // EB
    squares = jnp.sum(jnp.square(train_grads.astype(F32)), axis=1)
    scale = lax.rsqrt(squares + EPSILON)[None, :]
    order, count = pair_eval[index], pair_count[index]
    hits = order[:, None] == jnp.arange(blocks, dtype=jnp.int32)[None, :]
    inside = jnp.arange(order.shape[0], dtype=jnp.int32)[:, None] < count
    flags = jnp.any(hits & inside, axis=0).astype(jnp.int32)
    return scores(flags, evals, hi, lo, train_grads, scale)


def solution(mesh):
    placed = (P(("groups", "dp"), None), P(("groups", "dp"), None), P("groups", None), P("groups"))
    return jax.shard_map(
        functools.partial(per_device, n=mesh.shape["dp"]),
        mesh=mesh,
        in_specs=placed,
        out_specs=P(None, ("groups", "dp")),
        check_vma=False,
    )
```

```python
import functools

import jax
import jax.numpy as jnp
from jax import lax
from jax.experimental import pallas as pl
from jax.experimental.pallas import tpu as pltpu
from jax.sharding import PartitionSpec as P

EB = 256
DAMPING = 0.1
EPSILON = 1e-06
B = 128
F32, BF16 = jnp.float32, jnp.bfloat16
NT = (((1,), (1,)), ((), ()))
NN = (((1,), (0,)), ((), ()))
TN = (((0,), (0,)), ((), ()))
VMEM_BYTES = 56 * 1024 * 1024


def dot(a, b, dims):
    return lax.dot_general(a, b, dims, preferred_element_type=F32)


def slab_offset(j, nb):
    return B * (j * nb - j * (j - 1) // 2)


def split3(x):
    hi = x.astype(BF16)
    rest = x - hi.astype(F32)
    mid = rest.astype(BF16)
    lo = (rest - mid.astype(F32)).astype(BF16)
    return hi, mid, lo


def left_parts(x):
    h, m, l = split3(x)
    return jnp.concatenate([h, h, m, m, h, l], axis=1)


def right_parts(x, axis=1):
    h, m, l = split3(x)
    return jnp.concatenate([h, m, h, m, l, h], axis=axis)


def chunk_plan(nb, pieces):
    cut = max(nb // 4, 1)
    plan = []
    for first, last in ((0, cut), (cut, nb)):
        start, stop = slab_offset(first, nb), slab_offset(last, nb)
        rows = -(-(stop - start) // (8 * pieces)) * 8
        plan.append((first, last, start, rows))
    return plan


def gram_kernel(me_ref, t_ref, *refs, nb, pieces):
    width = nb * B
    plan = chunk_plan(nb, pieces)
    outs, packs = refs[: 2 * len(plan)], refs[2 * len(plan) :]

    def chunk_of(j):
        return next(c for c, p in enumerate(plan) if p[0] <= j < p[1])

    for J in range(nb // 2):
        c0 = 2 * B * J
        g = dot(t_ref[:, c0:], t_ref[:, c0 : c0 + 2 * B], TN)
        for h in range(2):
            j = 2 * J + h
            c = chunk_of(j)
            o = slab_offset(j, nb) - plan[c][2]
            packs[c][o : o + width - B * j, :] = g[B * h :, B * h : B * h + B]
    me = me_ref[0]
    half = pieces // 2
    for c, (first, last, start, rows) in enumerate(plan):
        used = slab_offset(last, nb) - start
        if used < pieces * rows:
            packs[c][used:, :] = jnp.zeros((pieces * rows - used, B), F32)
        for q in range(pieces):
            at = pl.multiple_of((me ^ q) * rows, 8)
            out = outs[2 * c + q // half]
            q = q % half
            out[q * rows : (q + 1) * rows, :] = packs[c][pl.ds(at, rows), :]


def local_gram(me, t, pieces):
    nb = t.shape[1] // B
    plan = chunk_plan(nb, pieces)
    halves = [jax.ShapeDtypeStruct((pieces // 2 * p[3], B), F32) for p in plan for _ in range(2)]
    return pl.pallas_call(
        functools.partial(gram_kernel, nb=nb, pieces=pieces),
        out_shape=halves,
        in_specs=[
            pl.BlockSpec(memory_space=pltpu.SMEM),
            pl.BlockSpec(memory_space=pltpu.VMEM),
        ],
        out_specs=[pl.BlockSpec(memory_space=pltpu.VMEM) for _ in halves],
        scratch_shapes=[pltpu.VMEM((pieces * p[3], B), F32) for p in plan],
        compiler_params=pltpu.CompilerParams(vmem_limit_bytes=VMEM_BYTES),
        cost_estimate=pl.CostEstimate(
            flops=t.shape[0] * t.shape[1] * t.shape[1],
            bytes_accessed=t.size * 2 + sum(h.size for h in halves) * 4,
            transcendentals=0,
        ),
        name="local_gram",
    )(me, t)


def reduce_rows(S, R):
    S, R = [list(row) for row in S], list(R)

    def pivot(j, rc):
        s = {k: S[j][k] * rc for k in range(j + 1, 8)}
        row = R[j] * rc
        for i in range(8):
            if i == j:
                continue
            c = S[i][j] if i < j else S[j][i]
            for k in range(max(i, j + 1), 8):
                S[i][k] = S[i][k] - c * s[k]
            R[i] = R[i] - c * row
        for k in s:
            S[j][k] = s[k]
        R[j] = row

    for j in range(0, 8, 2):
        a, b, d = S[j][j], S[j][j + 1], S[j + 1][j + 1]
        rd = 1.0 / (a * d - b * b)
        pivot(j, 1.0 / a)
        pivot(j + 1, a * rd)
    return R


def invert_block(M, spread):
    M = list(M)
    full = (8, B)
    lane = lax.broadcasted_iota(jnp.int32, full, 1)
    sub = lax.broadcasted_iota(jnp.int32, full, 0)
    n = len(M)
    for b in range(n):
        k0 = 8 * b
        columns = lambda V: [jnp.broadcast_to(V[:, k0 + k : k0 + k + 1], full) for k in range(8)]
        base = 64 * (b % 2)
        for j, column in enumerate(columns(M[b])):
            spread[base + 8 * j : base + 8 * j + 8, :] = column
        S = [
            [None] * i + [spread[pl.ds(base + 8 * j + i, 8, stride=0), :] for j in range(i, 8)]
            for i in range(8)
        ]
        inside = (lane >= k0) & (lane < k0 + 8)
        R = [
            jnp.where(
                inside,
                jnp.where(lane == k0 + i, 1.0, 0.0).astype(F32),
                jnp.broadcast_to(M[b][i : i + 1, :], full),
            )
            for i in range(8)
        ]
        R = reduce_rows(S, R)
        for q in range(1, n + 1):
            t = (b + q) % n
            if t == b:
                x = R[0]
                for i in range(1, 8):
                    x = jnp.where(sub == i, R[i], x)
            else:
                c = columns(M[t])
                x, y = jnp.where(inside, 0.0, M[t]) - c[0] * R[0], c[1] * R[1]
                for k in (2, 4, 6):
                    x, y = x - c[k] * R[k], y + c[k + 1] * R[k + 1]
                x = x - y
            M[t] = x
    return M


def inverse_kernel(me_ref, *refs, nb, pieces):
    width = nb * B
    plan = chunk_plan(nb, pieces)
    count = len(plan)
    parts, (hi_ref, lo_ref), packs = refs[: 2 * count], refs[2 * count : 2 * count + 2], refs[2 * count + 2 : 3 * count + 2]
    A, D, inv, spread, W, WL, CL, CR = refs[3 * count + 2 :]
    me = me_ref[0]
    half = pieces // 2
    for c, (_, _, _, rows) in enumerate(plan):
        for q in range(pieces):
            to = pl.multiple_of((me ^ q) * rows, 8)
            p = q % half
            packs[c][pl.ds(to, rows), :] = parts[2 * c + q // half][p * rows : (p + 1) * rows, :]

    def column(j):
        c = next(c for c, p in enumerate(plan) if p[0] <= j < p[1])
        return packs[c], slab_offset(j, nb) - plan[c][2]

    eye = lax.broadcasted_iota(jnp.int32, (B, B), 0) == lax.broadcasted_iota(
        jnp.int32, (B, B), 1
    )
    diag = jnp.zeros((B, B), F32)
    for j in range(nb):
        pack, o = column(j)
        diag = diag + jnp.where(eye, pack[o : o + B, :], 0.0)
    trace = jnp.sum(jnp.sum(diag, axis=1, keepdims=True), axis=0, keepdims=True)
    scale = jnp.broadcast_to(width / trace, (1, B))
    damp = jnp.where(eye, DAMPING, 0.0).astype(F32)
    for j in range(nb):
        pack, o = column(j)
        A[j, B * j : B * j + B, :] = pack[o : o + B, :] * scale + damp
        if j + 1 < nb:
            A[j, B * j + B :, :] = pack[o + B : o + width - B * j, :] * scale
    MC = 256

    def split_column(k):
        for i in range(nb):
            x = A[k, B * i : B * i + B, :]
            x = jnp.where(k == i, jnp.zeros_like(x), x)
            CL[B * i : B * i + B, :] = left_parts(x)
            CR[B * i : B * i + B, :] = right_parts(x)

    def eliminate(k):
        pivot = inv[...]
        right = right_parts(pivot, axis=0)
        for i in range(nb):
            w = dot(CL[B * i : B * i + B, :], right, NN)
            w = jnp.where(k == i, -pivot, w)
            W[B * i : B * i + B, :] = w
            WL[B * i : B * i + B, :] = left_parts(w)
        for J in range(nb // 2):
            cols = CR[2 * B * J : 2 * B * (J + 1), :]
            for r in range(0, width, MC):
                u = dot(WL[r : r + MC, :], cols, NT)
                for h in range(2):
                    for q in range(0, MC, B):
                        at = slice(r + q, r + q + B)
                        x = A[2 * J + h, at, :]
                        x = jnp.where(k == (r + q) // B, jnp.zeros_like(x), x)
                        A[2 * J + h, at, :] = x - u[q : q + B, h * B : h * B + B]
        A[k] = W[...]

    def invert():
        return jnp.concatenate(
            invert_block([D[8 * t : 8 * t + 8, :] for t in range(B // 8)], spread)
        )

    def next_pivot(k):
        at = pl.ds(pl.multiple_of(k * B, B), B)
        w = dot(CL[at, :], right_parts(inv[...], axis=0), NN)
        D[...] = A[k, at, :] - dot(left_parts(w), CR[at, :], NT)

    D[...] = A[0, :B, :]
    split_column(0)
    inv[...] = invert()
    next_pivot(1)

    def step(k, carry):
        after = invert()
        eliminate(k)
        split_column(k + 1)
        inv[...] = after
        next_pivot(jnp.minimum(k + 2, nb - 1))
        return carry

    lax.fori_loop(0, nb - 1, step, 0)
    eliminate(nb - 1)
    for j in range(nb):
        x = -A[j]
        hi = x.astype(BF16)
        hi_ref[:, B * j : B * j + B] = hi
        lo_ref[:, B * j : B * j + B] = (x - hi.astype(F32)).astype(BF16)


def gram_inverse(me, parts, nb, pieces):
    width = nb * B
    out = jax.ShapeDtypeStruct((width, width), BF16)
    return pl.pallas_call(
        functools.partial(inverse_kernel, nb=nb, pieces=pieces),
        out_shape=(out, out),
        in_specs=[pl.BlockSpec(memory_space=pltpu.SMEM)]
        + [pl.BlockSpec(memory_space=pltpu.VMEM) for _ in parts],
        out_specs=(pl.BlockSpec(memory_space=pltpu.VMEM),) * 2,
        scratch_shapes=[pltpu.VMEM((pieces * p[3], B), F32) for p in chunk_plan(nb, pieces)]
        + [
            pltpu.VMEM((nb, width, B), F32),
            pltpu.VMEM((B, B), F32),
            pltpu.VMEM((B, B), F32),
            pltpu.VMEM((B, B), F32),
            pltpu.VMEM((width, B), F32),
            pltpu.VMEM((width, 6 * B), BF16),
            pltpu.VMEM((width, 6 * B), BF16),
            pltpu.VMEM((width, 6 * B), BF16),
        ],
        compiler_params=pltpu.CompilerParams(vmem_limit_bytes=VMEM_BYTES),
        cost_estimate=pl.CostEstimate(
            flops=12 * width**3, bytes_accessed=width * width * 8, transcendentals=0
        ),
        name="gram_inverse",
    )(me, *parts)


def score_kernel(me_ref, flag_ref, hi_ref, lo_ref, t_ref, scale_ref, *refs, rows):
    parts, out_ref, evals = refs[:-2], refs[-2], refs[-1]
    e = pl.program_id(0)

    @pl.when(e == 0)
    def _():
        for q2, part in enumerate(parts):
            for q in range(part.shape[0] // rows):
                owner = me_ref[0] ^ (q * len(parts) + q2)
                to = pl.multiple_of(owner * rows, 16)
                evals[pl.ds(to, rows), :] = part[q * rows : (q + 1) * rows, :]

    @pl.when(flag_ref[e] > 0)
    def _():
        block = evals[pl.ds(pl.multiple_of(e * EB, EB), EB), :]
        pre = (dot(block, hi_ref[...], NN) + dot(block, lo_ref[...], NN)).astype(BF16)
        score = dot(pre, t_ref[...], NT)
        out_ref[pl.ds(e, 1), :] = jnp.max(score, axis=0, keepdims=True) * scale_ref[...]

    @pl.when(flag_ref[e] <= 0)
    def _():
        out_ref[pl.ds(e, 1), :] = jnp.zeros((1, out_ref.shape[1]), F32)


def scores(index, flags, parts, rows, hi, lo, t, scale):
    total = sum(p.shape[0] for p in parts)
    blocks = total // EB
    width = t.shape[1]
    whole = lambda shape: pl.BlockSpec(shape, lambda e: (0, 0))
    smem = pl.BlockSpec(memory_space=pltpu.SMEM)
    operands = (hi, lo, t, scale) + tuple(parts)
    return pl.pallas_call(
        functools.partial(score_kernel, rows=rows),
        grid=(blocks,),
        out_shape=jax.ShapeDtypeStruct((blocks, t.shape[0]), F32),
        in_specs=[smem, smem] + [whole(x.shape) for x in operands],
        out_specs=whole((blocks, t.shape[0])),
        scratch_shapes=[pltpu.VMEM((total, width), BF16)],
        compiler_params=pltpu.CompilerParams(vmem_limit_bytes=VMEM_BYTES),
        cost_estimate=pl.CostEstimate(
            flops=6 * total * width * width,
            bytes_accessed=total * width * 2 + width * width * 6,
            transcendentals=0,
        ),
        name="scores",
    )(index, flags, *operands)


def bit_groups(n):
    bits = [1 << s for s in range(n.bit_length() - 1)]
    groups = [[b] for b in bits[:2]]
    rest = bits[2:]
    while rest:
        groups.append(rest[:2])
        rest = rest[2:]
    return groups


def send(x, mask, n):
    return lax.ppermute(x, "dp", [(i, i ^ mask) for i in range(n)])


def place_of(index, n):
    place, step = 0, n
    for group in bit_groups(n):
        size = 1 << len(group)
        step //= size
        place = place + (index // group[0]) % size * step
    return place


def spread_out(x, group, n):
    return [x] + [send(x, q * group[0], n) for q in range(1, 1 << len(group))]


def all_reduce(chunks, n):
    groups = bit_groups(n)
    chunks = [keep + send(other, groups[0][0], n) for keep, other in chunks]
    for group in groups[1:]:
        size = 1 << len(group)
        after = []
        for x in chunks:
            part = x.shape[0] // size
            total = x[:part]
            for q in range(1, size):
                total = total + send(x[q * part : (q + 1) * part], q * group[0], n)
            after.append(total)
        chunks = after
    for group in reversed(groups[1:]):
        chunks = [jnp.concatenate(spread_out(x, group, n)) for x in chunks]
    return [(x, send(x, groups[0][0], n)) for x in chunks]


def per_device(train_grads, eval_grads, pair_eval, pair_count, n):
    width = train_grads.shape[1]
    nb = width // B
    index = lax.axis_index("dp")
    evals = eval_grads
    for group in bit_groups(n)[2:]:
        evals = jnp.concatenate(spread_out(evals, group, n))
    me = place_of(index, n)[None]
    halves = local_gram(me, train_grads, n)
    chunks = all_reduce(list(zip(halves[::2], halves[1::2])), n)
    chunks, evals = lax.optimization_barrier((chunks, evals))
    parts = spread_out(evals, [1, 2], n)
    hi, lo = gram_inverse(me, [x for pair in chunks for x in pair], nb, n)
    blocks = eval_grads.shape[0] * n // EB
    squares = jnp.sum(jnp.square(train_grads.astype(F32)), axis=1)
    scale = lax.rsqrt(squares + EPSILON)[None, :]
    order, count = pair_eval[index], pair_count[index]
    hits = order[:, None] == jnp.arange(blocks, dtype=jnp.int32)[None, :]
    inside = jnp.arange(order.shape[0], dtype=jnp.int32)[:, None] < count
    flags = jnp.any(hits & inside, axis=0).astype(jnp.int32)
    return scores(index[None], flags, parts, eval_grads.shape[0], hi, lo, train_grads, scale)


def solution(mesh):
    placed = (P(("groups", "dp"), None), P(("groups", "dp"), None), P("groups", None), P("groups"))
    return jax.shard_map(
        functools.partial(per_device, n=mesh.shape["dp"]),
        mesh=mesh,
        in_specs=placed,
        out_specs=P(None, ("groups", "dp")),
        check_vma=False,
    )
```

```python
import functools

import jax
import jax.numpy as jnp
from jax import lax
from jax.experimental import pallas as pl
from jax.experimental.pallas import tpu as pltpu
from jax.sharding import PartitionSpec as P

EB = 256
DAMPING = 0.1
EPSILON = 1e-06
B = 128
F32, BF16 = jnp.float32, jnp.bfloat16
NT = (((1,), (1,)), ((), ()))
NN = (((1,), (0,)), ((), ()))
TN = (((0,), (0,)), ((), ()))
MIB = 1024 * 1024


def dot(a, b, dims):
    return lax.dot_general(a, b, dims, preferred_element_type=F32)


def slab_offset(j, nb):
    return B * (j * nb - j * (j - 1) // 2)


def split3(x):
    hi = x.astype(BF16)
    rest = x - hi.astype(F32)
    mid = rest.astype(BF16)
    lo = (rest - mid.astype(F32)).astype(BF16)
    return hi, mid, lo


def left_parts(x):
    h, m, l = split3(x)
    return jnp.concatenate([h, h, m, m, h, l], axis=1)


def right_parts(x, axis=1):
    h, m, l = split3(x)
    return jnp.concatenate([h, m, h, m, l, h], axis=axis)


def chunk_plan(nb, pieces):
    cut = max(nb // 4, 1)
    plan = []
    for first, last in ((0, cut), (cut, nb)):
        start, stop = slab_offset(first, nb), slab_offset(last, nb)
        rows = -(-(stop - start) // (8 * pieces)) * 8
        plan.append((first, last, start, rows))
    return plan


def gram_kernel(me_ref, t_ref, *refs, nb, pieces):
    width = nb * B
    plan = chunk_plan(nb, pieces)
    outs, packs = refs[: 2 * len(plan)], refs[2 * len(plan) :]

    def chunk_of(j):
        return next(c for c, p in enumerate(plan) if p[0] <= j < p[1])

    for J in range(nb // 2):
        c0 = 2 * B * J
        g = dot(t_ref[:, c0:], t_ref[:, c0 : c0 + 2 * B], TN)
        for h in range(2):
            j = 2 * J + h
            c = chunk_of(j)
            o = slab_offset(j, nb) - plan[c][2]
            packs[c][o : o + width - B * j, :] = g[B * h :, B * h : B * h + B]
    half = pieces // 2
    for c, (first, last, start, rows) in enumerate(plan):
        me = me_ref[c]
        used = slab_offset(last, nb) - start
        if used < pieces * rows:
            packs[c][used:, :] = jnp.zeros((pieces * rows - used, B), F32)
        for q in range(pieces):
            at = pl.multiple_of((me ^ q) * rows, 8)
            out = outs[2 * c + q // half]
            q = q % half
            out[q * rows : (q + 1) * rows, :] = packs[c][pl.ds(at, rows), :]


def local_gram(me, t, pieces):
    nb = t.shape[1] // B
    plan = chunk_plan(nb, pieces)
    halves = [jax.ShapeDtypeStruct((pieces // 2 * p[3], B), F32) for p in plan for _ in range(2)]
    return pl.pallas_call(
        functools.partial(gram_kernel, nb=nb, pieces=pieces),
        out_shape=halves,
        in_specs=[
            pl.BlockSpec(memory_space=pltpu.SMEM),
            pl.BlockSpec(memory_space=pltpu.VMEM),
        ],
        out_specs=[pl.BlockSpec(memory_space=pltpu.VMEM) for _ in halves],
        scratch_shapes=[pltpu.VMEM((pieces * p[3], B), F32) for p in plan],
        compiler_params=pltpu.CompilerParams(vmem_limit_bytes=24 * MIB),
        cost_estimate=pl.CostEstimate(
            flops=t.shape[0] * t.shape[1] * t.shape[1],
            bytes_accessed=t.size * 2 + sum(h.size for h in halves) * 4,
            transcendentals=0,
        ),
        name="local_gram",
    )(me, t)


def reduce_rows(S, R):
    S, R = [list(row) for row in S], list(R)

    def pivot(j, rc):
        s = {k: S[j][k] * rc for k in range(j + 1, 8)}
        row = R[j] * rc
        for i in range(8):
            if i == j:
                continue
            c = S[i][j] if i < j else S[j][i]
            for k in range(max(i, j + 1), 8):
                S[i][k] = S[i][k] - c * s[k]
            R[i] = R[i] - c * row
        for k in s:
            S[j][k] = s[k]
        R[j] = row

    for j in range(0, 8, 2):
        a, b, d = S[j][j], S[j][j + 1], S[j + 1][j + 1]
        rd = 1.0 / (a * d - b * b)
        pivot(j, 1.0 / a)
        pivot(j + 1, a * rd)
    return R


def invert_block(M, spread):
    M = list(M)
    full = (8, B)
    lane = lax.broadcasted_iota(jnp.int32, full, 1)
    sub = lax.broadcasted_iota(jnp.int32, full, 0)
    n = len(M)
    for b in range(n):
        k0 = 8 * b
        columns = lambda V: [jnp.broadcast_to(V[:, k0 + k : k0 + k + 1], full) for k in range(8)]
        base = 64 * (b % 2)
        for j, column in enumerate(columns(M[b])):
            spread[base + 8 * j : base + 8 * j + 8, :] = column
        S = [
            [None] * i + [spread[pl.ds(base + 8 * j + i, 8, stride=0), :] for j in range(i, 8)]
            for i in range(8)
        ]
        inside = (lane >= k0) & (lane < k0 + 8)
        R = [
            jnp.where(
                inside,
                jnp.where(lane == k0 + i, 1.0, 0.0).astype(F32),
                jnp.broadcast_to(M[b][i : i + 1, :], full),
            )
            for i in range(8)
        ]
        R = reduce_rows(S, R)
        for q in range(1, n + 1):
            t = (b + q) % n
            if t == b:
                x = R[0]
                for i in range(1, 8):
                    x = jnp.where(sub == i, R[i], x)
            else:
                c = columns(M[t])
                x, y = jnp.where(inside, 0.0, M[t]) - c[0] * R[0], c[1] * R[1]
                for k in (2, 4, 6):
                    x, y = x - c[k] * R[k], y + c[k + 1] * R[k + 1]
                x = x - y
            M[t] = x
    return M


def inverse_kernel(me_ref, *refs, nb, pieces):
    width = nb * B
    plan = chunk_plan(nb, pieces)
    count = len(plan)
    parts, (hi_ref, lo_ref), packs = refs[: 2 * count], refs[2 * count : 2 * count + 2], refs[2 * count + 2 : 3 * count + 2]
    A, D, inv, spread, W, WL, CL, CR = refs[3 * count + 2 :]
    half = pieces // 2
    for c, (_, _, _, rows) in enumerate(plan):
        me = me_ref[c]
        for q in range(pieces):
            to = pl.multiple_of((me ^ q) * rows, 8)
            p = q % half
            packs[c][pl.ds(to, rows), :] = parts[2 * c + q // half][p * rows : (p + 1) * rows, :]

    def column(j):
        c = next(c for c, p in enumerate(plan) if p[0] <= j < p[1])
        return packs[c], slab_offset(j, nb) - plan[c][2]

    eye = lax.broadcasted_iota(jnp.int32, (B, B), 0) == lax.broadcasted_iota(
        jnp.int32, (B, B), 1
    )
    diag = jnp.zeros((B, B), F32)
    for j in range(nb):
        pack, o = column(j)
        diag = diag + jnp.where(eye, pack[o : o + B, :], 0.0)
    trace = jnp.sum(jnp.sum(diag, axis=1, keepdims=True), axis=0, keepdims=True)
    scale = jnp.broadcast_to(width / trace, (1, B))
    damp = jnp.where(eye, DAMPING, 0.0).astype(F32)
    for j in range(nb):
        pack, o = column(j)
        A[j, B * j : B * j + B, :] = pack[o : o + B, :] * scale + damp
        if j + 1 < nb:
            A[j, B * j + B :, :] = pack[o + B : o + width - B * j, :] * scale
    MC = 256

    def split_column(k):
        for i in range(nb):
            x = A[k, B * i : B * i + B, :]
            x = jnp.where(k == i, jnp.zeros_like(x), x)
            CL[B * i : B * i + B, :] = left_parts(x)
            CR[B * i : B * i + B, :] = right_parts(x)

    def eliminate(k):
        pivot = inv[...]
        right = right_parts(pivot, axis=0)
        for i in range(nb):
            w = dot(CL[B * i : B * i + B, :], right, NN)
            w = jnp.where(k == i, -pivot, w)
            W[B * i : B * i + B, :] = w
            WL[B * i : B * i + B, :] = left_parts(w)
        for J in range(nb // 2):
            cols = CR[2 * B * J : 2 * B * (J + 1), :]
            for r in range(0, width, MC):
                u = dot(WL[r : r + MC, :], cols, NT)
                for h in range(2):
                    for q in range(0, MC, B):
                        at = slice(r + q, r + q + B)
                        x = A[2 * J + h, at, :]
                        x = jnp.where(k == (r + q) // B, jnp.zeros_like(x), x)
                        A[2 * J + h, at, :] = x - u[q : q + B, h * B : h * B + B]
        A[k] = W[...]

    def invert():
        return jnp.concatenate(
            invert_block([D[8 * t : 8 * t + 8, :] for t in range(B // 8)], spread)
        )

    def next_pivot(k):
        at = pl.ds(pl.multiple_of(k * B, B), B)
        w = dot(CL[at, :], right_parts(inv[...], axis=0), NN)
        D[...] = A[k, at, :] - dot(left_parts(w), CR[at, :], NT)

    D[...] = A[0, :B, :]
    split_column(0)
    inv[...] = invert()
    next_pivot(1)

    def step(k, carry):
        after = invert()
        eliminate(k)
        split_column(k + 1)
        inv[...] = after
        next_pivot(jnp.minimum(k + 2, nb - 1))
        return carry

    lax.fori_loop(0, nb - 1, step, 0)
    eliminate(nb - 1)
    for j in range(nb):
        x = -A[j]
        hi = x.astype(BF16)
        hi_ref[:, B * j : B * j + B] = hi
        lo_ref[:, B * j : B * j + B] = (x - hi.astype(F32)).astype(BF16)


def gram_inverse(me, parts, nb, pieces):
    width = nb * B
    out = jax.ShapeDtypeStruct((width, width), BF16)
    return pl.pallas_call(
        functools.partial(inverse_kernel, nb=nb, pieces=pieces),
        out_shape=(out, out),
        in_specs=[pl.BlockSpec(memory_space=pltpu.SMEM)]
        + [pl.BlockSpec(memory_space=pltpu.VMEM) for _ in parts],
        out_specs=(pl.BlockSpec(memory_space=pltpu.VMEM),) * 2,
        scratch_shapes=[pltpu.VMEM((pieces * p[3], B), F32) for p in chunk_plan(nb, pieces)]
        + [
            pltpu.VMEM((nb, width, B), F32),
            pltpu.VMEM((B, B), F32),
            pltpu.VMEM((B, B), F32),
            pltpu.VMEM((B, B), F32),
            pltpu.VMEM((width, B), F32),
            pltpu.VMEM((width, 6 * B), BF16),
            pltpu.VMEM((width, 6 * B), BF16),
            pltpu.VMEM((width, 6 * B), BF16),
        ],
        compiler_params=pltpu.CompilerParams(vmem_limit_bytes=32 * MIB),
        cost_estimate=pl.CostEstimate(
            flops=12 * width**3, bytes_accessed=width * width * 8, transcendentals=0
        ),
        name="gram_inverse",
    )(me, *parts)


def score_kernel(me_ref, flag_ref, hi_ref, lo_ref, t_ref, scale_ref, *refs, rows, masks):
    parts, out_ref, evals = refs[:-2], refs[-2], refs[-1]
    e = pl.program_id(0)

    @pl.when(e == 0)
    def _():
        for part, held in zip(parts, masks):
            for q, mask in enumerate(held):
                to = pl.multiple_of((me_ref[0] ^ mask) * rows, 16)
                evals[pl.ds(to, rows), :] = part[q * rows : (q + 1) * rows, :]

    @pl.when(flag_ref[e] > 0)
    def _():
        block = evals[pl.ds(pl.multiple_of(e * EB, EB), EB), :]
        pre = (dot(block, hi_ref[...], NN) + dot(block, lo_ref[...], NN)).astype(BF16)
        score = dot(pre, t_ref[...], NT)
        out_ref[pl.ds(e, 1), :] = jnp.max(score, axis=0, keepdims=True) * scale_ref[...]

    @pl.when(flag_ref[e] <= 0)
    def _():
        out_ref[pl.ds(e, 1), :] = jnp.zeros((1, out_ref.shape[1]), F32)


def scores(index, flags, parts, masks, rows, hi, lo, t, scale):
    total = sum(p.shape[0] for p in parts)
    blocks = total // EB
    width = t.shape[1]
    whole = lambda shape: pl.BlockSpec(shape, lambda e: (0, 0))
    smem = pl.BlockSpec(memory_space=pltpu.SMEM)
    operands = (hi, lo, t, scale) + tuple(parts)
    return pl.pallas_call(
        functools.partial(score_kernel, rows=rows, masks=masks),
        grid=(blocks,),
        out_shape=jax.ShapeDtypeStruct((blocks, t.shape[0]), F32),
        in_specs=[smem, smem] + [whole(x.shape) for x in operands],
        out_specs=whole((blocks, t.shape[0])),
        scratch_shapes=[pltpu.VMEM((total, width), BF16)],
        compiler_params=pltpu.CompilerParams(vmem_limit_bytes=20 * MIB + 8 * total * width),
        cost_estimate=pl.CostEstimate(
            flops=6 * total * width * width,
            bytes_accessed=total * width * 2 + width * width * 6,
            transcendentals=0,
        ),
        name="scores",
    )(index, flags, *operands)


def bit_groups(n):
    bits = [1 << s for s in range(n.bit_length() - 1)]
    groups = [[b] for b in bits[:2]]
    rest = bits[2:]
    while rest:
        groups.append(rest[:2])
        rest = rest[2:]
    return groups


def send(x, mask, n):
    return lax.ppermute(x, "dp", [(i, i ^ mask) for i in range(n)])


def exchange_orders(n):
    groups = bit_groups(n)
    return [groups[:1] + groups[:0:-1], groups]


def place_of(index, order, n):
    place, step = 0, n
    for group in order:
        size = 1 << len(group)
        step //= size
        place = place + (index // group[0]) % size * step
    return place


def spread_out(x, group, n):
    return [x] + [send(x, q * group[0], n) for q in range(1, 1 << len(group))]


def gather_stage(x, masks, group, n):
    steps = [q * group[0] for q in range(1 << len(group))]
    return jnp.concatenate(spread_out(x, group, n)), [m ^ step for step in steps for m in masks]


def all_reduce(chunks, evals, orders, n):
    first = orders[0][0][0]
    chunks = [keep + send(other, first, n) for keep, other in chunks]
    groups, masks = bit_groups(n), [0]
    for group in groups[1:2] + groups[3:]:
        evals, masks = gather_stage(evals, masks, group, n)
    stages = len(orders[0])
    for s in range(1, stages):
        after = []
        for x, order in zip(chunks, orders):
            size = 1 << len(order[s])
            part = x.shape[0] // size
            total = x[:part]
            for q in range(1, size):
                total = total + send(x[q * part : (q + 1) * part], q * order[s][0], n)
            after.append(total)
        chunks, evals = lax.optimization_barrier((after, evals))
    for s in range(stages - 1, 0, -1):
        chunks = [
            jnp.concatenate(spread_out(x, order[s], n)) for x, order in zip(chunks, orders)
        ]
        chunks = lax.optimization_barrier(chunks)
    return [(x, send(x, first, n)) for x in chunks], evals, masks


def per_device(train_grads, eval_grads, pair_eval, pair_count, n):
    width = train_grads.shape[1]
    nb = width // B
    index = lax.axis_index("dp")
    orders = exchange_orders(n)
    me = jnp.stack([place_of(index, order, n) for order in orders])
    halves = local_gram(me, train_grads, n)
    chunks, evals, masks = all_reduce(
        list(zip(halves[::2], halves[1::2])), eval_grads, orders, n
    )
    chunks, evals = lax.optimization_barrier((chunks, evals))
    groups = bit_groups(n)
    for group in groups[2:3]:
        evals, masks = gather_stage(evals, masks, group, n)
    hi, lo = gram_inverse(me, [x for pair in chunks for x in pair], nb, n)
    evals, hi = lax.optimization_barrier((evals, hi))
    parts = spread_out(evals, groups[0], n)
    masks = [masks, [m ^ groups[0][0] for m in masks]]
    blocks = eval_grads.shape[0] * n // EB
    squares = jnp.sum(jnp.square(train_grads.astype(F32)), axis=1)
    scale = lax.rsqrt(squares + EPSILON)[None, :]
    order, count = pair_eval[index], pair_count[index]
    hits = order[:, None] == jnp.arange(blocks, dtype=jnp.int32)[None, :]
    inside = jnp.arange(order.shape[0], dtype=jnp.int32)[:, None] < count
    flags = jnp.any(hits & inside, axis=0).astype(jnp.int32)
    return scores(index[None], flags, parts, masks, eval_grads.shape[0], hi, lo, train_grads, scale)


def solution(mesh):
    placed = (P(("groups", "dp"), None), P(("groups", "dp"), None), P("groups", None), P("groups"))
    return jax.shard_map(
        functools.partial(per_device, n=mesh.shape["dp"]),
        mesh=mesh,
        in_specs=placed,
        out_specs=P(None, ("groups", "dp")),
        check_vma=False,
    )
```

```python
import functools

import jax
import jax.numpy as jnp
from jax import lax
from jax.experimental import pallas as pl
from jax.experimental.pallas import tpu as pltpu
from jax.sharding import PartitionSpec as P

EB = 256
DAMPING = 0.1
EPSILON = 1e-06
B = 128
F32, BF16 = jnp.float32, jnp.bfloat16
NT = (((1,), (1,)), ((), ()))
NN = (((1,), (0,)), ((), ()))
TN = (((0,), (0,)), ((), ()))
MIB = 1024 * 1024


def dot(a, b, dims):
    return lax.dot_general(a, b, dims, preferred_element_type=F32)


def slab_offset(j, nb):
    return B * (j * nb - j * (j - 1) // 2)


def split3(x):
    hi = x.astype(BF16)
    rest = x - hi.astype(F32)
    mid = rest.astype(BF16)
    lo = (rest - mid.astype(F32)).astype(BF16)
    return hi, mid, lo


def left_parts(x):
    h, m, l = split3(x)
    return jnp.concatenate([h, h, m, m, h, l], axis=1)


def right_parts(x, axis=1):
    h, m, l = split3(x)
    return jnp.concatenate([h, m, h, m, l, h], axis=axis)


def chunk_plan(nb, pieces):
    cut = max(nb // 4, 1)
    plan = []
    for first, last in ((0, cut), (cut, nb)):
        start, stop = slab_offset(first, nb), slab_offset(last, nb)
        rows = -(-(stop - start) // (8 * pieces)) * 8
        plan.append((first, last, start, rows))
    return plan


def gram_kernel(me_ref, t_ref, *refs, nb, pieces):
    width = nb * B
    plan = chunk_plan(nb, pieces)
    outs, packs = refs[: 2 * len(plan)], refs[2 * len(plan) :]

    def chunk_of(j):
        return next(c for c, p in enumerate(plan) if p[0] <= j < p[1])

    for J in range(nb // 2):
        c0 = 2 * B * J
        g = dot(t_ref[:, c0:], t_ref[:, c0 : c0 + 2 * B], TN)
        for h in range(2):
            j = 2 * J + h
            c = chunk_of(j)
            o = slab_offset(j, nb) - plan[c][2]
            packs[c][o : o + width - B * j, :] = g[B * h :, B * h : B * h + B]
    half = pieces // 2
    for c, (first, last, start, rows) in enumerate(plan):
        me = me_ref[c]
        used = slab_offset(last, nb) - start
        if used < pieces * rows:
            packs[c][used:, :] = jnp.zeros((pieces * rows - used, B), F32)
        for q in range(pieces):
            at = pl.multiple_of((me ^ q) * rows, 8)
            out = outs[2 * c + q // half]
            q = q % half
            out[q * rows : (q + 1) * rows, :] = packs[c][pl.ds(at, rows), :]


def local_gram(me, t, pieces):
    nb = t.shape[1] // B
    plan = chunk_plan(nb, pieces)
    halves = [jax.ShapeDtypeStruct((pieces // 2 * p[3], B), F32) for p in plan for _ in range(2)]
    return pl.pallas_call(
        functools.partial(gram_kernel, nb=nb, pieces=pieces),
        out_shape=halves,
        in_specs=[
            pl.BlockSpec(memory_space=pltpu.SMEM),
            pl.BlockSpec(memory_space=pltpu.VMEM),
        ],
        out_specs=[pl.BlockSpec(memory_space=pltpu.VMEM) for _ in halves],
        scratch_shapes=[pltpu.VMEM((pieces * p[3], B), F32) for p in plan],
        compiler_params=pltpu.CompilerParams(vmem_limit_bytes=24 * MIB),
        cost_estimate=pl.CostEstimate(
            flops=t.shape[0] * t.shape[1] * t.shape[1],
            bytes_accessed=t.size * 2 + sum(h.size for h in halves) * 4,
            transcendentals=0,
        ),
        name="local_gram",
    )(me, t)


def reduce_rows(S, R):
    S, R = [list(row) for row in S], list(R)

    def pivot(j, rc):
        s = {k: S[j][k] * rc for k in range(j + 1, 8)}
        row = R[j] * rc
        for i in range(8):
            if i == j:
                continue
            c = S[i][j] if i < j else S[j][i]
            for k in range(max(i, j + 1), 8):
                S[i][k] = S[i][k] - c * s[k]
            R[i] = R[i] - c * row
        for k in s:
            S[j][k] = s[k]
        R[j] = row

    for j in range(0, 8, 2):
        a, b, d = S[j][j], S[j][j + 1], S[j + 1][j + 1]
        rd = 1.0 / (a * d - b * b)
        pivot(j, 1.0 / a)
        pivot(j + 1, a * rd)
    return R


def invert_block(M, spread):
    M = list(M)
    full = (8, B)
    lane = lax.broadcasted_iota(jnp.int32, full, 1)
    sub = lax.broadcasted_iota(jnp.int32, full, 0)
    zero = jnp.zeros(full, F32)
    n, panel = len(M), 8
    for p in range(0, n, panel):
        for b in range(p, p + panel):
            k0 = 8 * b
            columns = lambda V: [
                jnp.broadcast_to(V[:, k0 + k : k0 + k + 1], full) for k in range(8)
            ]
            base = 64 * (b % 2)
            for j, column in enumerate(columns(M[b])):
                spread[base + 8 * j : base + 8 * j + 8, :] = column
            S = [
                [None] * i + [spread[pl.ds(base + 8 * j + i, 8, stride=0), :] for j in range(i, 8)]
                for i in range(8)
            ]
            inside = (lane >= k0) & (lane < k0 + 8)
            R = [
                jnp.where(
                    inside,
                    jnp.where(lane == k0 + i, 1.0, 0.0).astype(F32),
                    jnp.broadcast_to(M[b][i : i + 1, :], full),
                )
                for i in range(8)
            ]
            R = reduce_rows(S, R)
            for q in range(1, panel + 1):
                t = p + (b - p + q) % panel
                if t == b:
                    x = R[0]
                    for i in range(1, 8):
                        x = jnp.where(sub == i, R[i], x)
                else:
                    c = columns(M[t])
                    x, y = jnp.where(inside, 0.0, M[t]) - c[0] * R[0], c[1] * R[1]
                    for k in (2, 4, 6):
                        x, y = x - c[k] * R[k], y + c[k + 1] * R[k + 1]
                    x = x - y
                M[t] = x
        own = range(p, p + panel)
        wide = (lane >= 8 * p) & (lane < 8 * (p + panel))
        C = jnp.concatenate([zero if t in own else jnp.where(wide, M[t], 0.0) for t in range(n)])
        R = jnp.concatenate([M[t] if t in own else zero for t in range(n)])
        U = dot(left_parts(C), right_parts(R, axis=0), NN)
        for t in range(n):
            if t not in own:
                M[t] = jnp.where(wide, 0.0, M[t]) - U[8 * t : 8 * t + 8, :]
    return M


def inverse_kernel(me_ref, *refs, nb, pieces):
    width = nb * B
    plan = chunk_plan(nb, pieces)
    count = len(plan)
    parts, (hi_ref, lo_ref, end_ref) = refs[: 2 * count], refs[2 * count : 2 * count + 3]
    packs = refs[2 * count + 3 : 3 * count + 3]
    A, D, inv, spread, W, WL, CL, CR = refs[3 * count + 3 :]
    half = pieces // 2
    for c, (_, _, _, rows) in enumerate(plan):
        me = me_ref[c]
        for q in range(pieces):
            to = pl.multiple_of((me ^ q) * rows, 8)
            p = q % half
            packs[c][pl.ds(to, rows), :] = parts[2 * c + q // half][p * rows : (p + 1) * rows, :]

    def column(j):
        c = next(c for c, p in enumerate(plan) if p[0] <= j < p[1])
        return packs[c], slab_offset(j, nb) - plan[c][2]

    eye = lax.broadcasted_iota(jnp.int32, (B, B), 0) == lax.broadcasted_iota(
        jnp.int32, (B, B), 1
    )
    diag = jnp.zeros((B, B), F32)
    for j in range(nb):
        pack, o = column(j)
        diag = diag + jnp.where(eye, pack[o : o + B, :], 0.0)
    trace = jnp.sum(jnp.sum(diag, axis=1, keepdims=True), axis=0, keepdims=True)
    scale = jnp.broadcast_to(width / trace, (1, B))
    damp = jnp.where(eye, DAMPING, 0.0).astype(F32)
    for j in range(nb):
        pack, o = column(j)
        A[j, B * j : B * j + B, :] = pack[o : o + B, :] * scale + damp
        if j + 1 < nb:
            A[j, B * j + B :, :] = pack[o + B : o + width - B * j, :] * scale
    MC = 256

    def split_column(k):
        for i in range(nb):
            x = A[k, B * i : B * i + B, :]
            x = jnp.where(k == i, jnp.zeros_like(x), x)
            CL[B * i : B * i + B, :] = left_parts(x)
            CR[B * i : B * i + B, :] = right_parts(x)

    def eliminate(k):
        pivot = inv[...]
        right = right_parts(pivot, axis=0)
        for i in range(nb):
            w = dot(CL[B * i : B * i + B, :], right, NN)
            w = jnp.where(k == i, -pivot, w)
            W[B * i : B * i + B, :] = w
            WL[B * i : B * i + B, :] = left_parts(w)
        for J in range(nb // 2):
            cols = CR[2 * B * J : 2 * B * (J + 1), :]
            for r in range(0, width, MC):
                u = dot(WL[r : r + MC, :], cols, NT)
                for h in range(2):
                    for q in range(0, MC, B):
                        at = slice(r + q, r + q + B)
                        x = A[2 * J + h, at, :]
                        x = jnp.where(k == (r + q) // B, jnp.zeros_like(x), x)
                        A[2 * J + h, at, :] = x - u[q : q + B, h * B : h * B + B]
        A[k] = W[...]

    def invert():
        return jnp.concatenate(
            invert_block([D[8 * t : 8 * t + 8, :] for t in range(B // 8)], spread)
        )

    def next_pivot(k):
        at = pl.ds(pl.multiple_of(k * B, B), B)
        w = dot(CL[at, :], right_parts(inv[...], axis=0), NN)
        D[...] = A[k, at, :] - dot(left_parts(w), CR[at, :], NT)

    D[...] = A[0, :B, :]
    split_column(0)
    inv[...] = invert()
    next_pivot(1)

    def step(k, carry):
        eliminate(k)
        split_column(k + 1)
        after = invert()
        inv[...] = after
        next_pivot(jnp.minimum(k + 2, nb - 1))
        return carry

    lax.fori_loop(0, nb - 1, step, 0)
    eliminate(nb - 1)
    end_ref[...] = jnp.zeros_like(end_ref)
    for j in range(nb):
        x = -A[j]
        hi = x.astype(BF16)
        hi_ref[:, B * j : B * j + B] = hi
        lo_ref[:, B * j : B * j + B] = (x - hi.astype(F32)).astype(BF16)


def gram_inverse(me, parts, nb, pieces):
    width = nb * B
    out = jax.ShapeDtypeStruct((width, width), BF16)
    return pl.pallas_call(
        functools.partial(inverse_kernel, nb=nb, pieces=pieces),
        out_shape=(out, out, jax.ShapeDtypeStruct((8, B), F32)),
        in_specs=[pl.BlockSpec(memory_space=pltpu.SMEM)]
        + [pl.BlockSpec(memory_space=pltpu.VMEM) for _ in parts],
        out_specs=(pl.BlockSpec(memory_space=pltpu.VMEM),) * 3,
        scratch_shapes=[pltpu.VMEM((pieces * p[3], B), F32) for p in chunk_plan(nb, pieces)]
        + [
            pltpu.VMEM((nb, width, B), F32),
            pltpu.VMEM((B, B), F32),
            pltpu.VMEM((B, B), F32),
            pltpu.VMEM((B, B), F32),
            pltpu.VMEM((width, B), F32),
            pltpu.VMEM((width, 6 * B), BF16),
            pltpu.VMEM((width, 6 * B), BF16),
            pltpu.VMEM((width, 6 * B), BF16),
        ],
        compiler_params=pltpu.CompilerParams(vmem_limit_bytes=32 * MIB),
        cost_estimate=pl.CostEstimate(
            flops=24 * width**3, bytes_accessed=width * width * 8, transcendentals=0
        ),
        name="gram_inverse",
    )(me, *parts)


def score_kernel(me_ref, flag_ref, hi_ref, lo_ref, t_ref, scale_ref, end_ref, *refs, rows, masks):
    parts, out_ref, evals = refs[:-2], refs[-2], refs[-1]
    e = pl.program_id(0)

    @pl.when(e == 0)
    def _():
        for part, held in zip(parts, masks):
            for q, mask in enumerate(held):
                to = pl.multiple_of((me_ref[0] ^ mask) * rows, 16)
                evals[pl.ds(to, rows), :] = part[q * rows : (q + 1) * rows, :]

    @pl.when(flag_ref[e] > 0)
    def _():
        block = evals[pl.ds(pl.multiple_of(e * EB, EB), EB), :]
        pre = (dot(block, hi_ref[...], NN) + dot(block, lo_ref[...], NN)).astype(BF16)
        score = dot(pre, t_ref[...], NT)
        out_ref[pl.ds(e, 1), :] = jnp.max(score, axis=0, keepdims=True) * scale_ref[...]

    @pl.when(flag_ref[e] <= 0)
    def _():
        out_ref[pl.ds(e, 1), :] = jnp.zeros((1, out_ref.shape[1]), F32)


def scores(index, flags, parts, masks, rows, hi, lo, t, scale, end):
    total = sum(p.shape[0] for p in parts)
    blocks = total // EB
    width = t.shape[1]
    whole = lambda shape: pl.BlockSpec(shape, lambda e: (0, 0))
    smem = pl.BlockSpec(memory_space=pltpu.SMEM)
    operands = (hi, lo, t, scale, end) + tuple(parts)
    return pl.pallas_call(
        functools.partial(score_kernel, rows=rows, masks=masks),
        grid=(blocks,),
        out_shape=jax.ShapeDtypeStruct((blocks, t.shape[0]), F32),
        in_specs=[smem, smem] + [whole(x.shape) for x in operands],
        out_specs=whole((blocks, t.shape[0])),
        scratch_shapes=[pltpu.VMEM((total, width), BF16)],
        compiler_params=pltpu.CompilerParams(vmem_limit_bytes=20 * MIB + 8 * total * width),
        cost_estimate=pl.CostEstimate(
            flops=6 * total * width * width,
            bytes_accessed=total * width * 2 + width * width * 6,
            transcendentals=0,
        ),
        name="scores",
    )(index, flags, *operands)


def bit_groups(n):
    bits = [1 << s for s in range(n.bit_length() - 1)]
    groups = [[b] for b in bits[:2]]
    rest = bits[2:]
    while rest:
        groups.append(rest[:2])
        rest = rest[2:]
    return groups


def send(x, mask, n):
    return lax.ppermute(x, "dp", [(i, i ^ mask) for i in range(n)])


def exchange_orders(n):
    groups = bit_groups(n)
    return [groups[:1] + groups[:0:-1], groups]


def place_of(index, order, n):
    place, step = 0, n
    for group in order:
        size = 1 << len(group)
        step //= size
        place = place + (index // group[0]) % size * step
    return place


def spread_out(x, group, n):
    return [x] + [send(x, q * group[0], n) for q in range(1, 1 << len(group))]


def gather_stage(x, masks, group, n):
    steps = [q * group[0] for q in range(1 << len(group))]
    return jnp.concatenate(spread_out(x, group, n)), [m ^ step for step in steps for m in masks]


def all_reduce(chunks, evals, orders, n):
    first = orders[0][0][0]
    chunks = [keep + send(other, first, n) for keep, other in chunks]
    groups, masks = bit_groups(n), [0]
    for group in groups[1:2] + groups[3:]:
        evals, masks = gather_stage(evals, masks, group, n)
    stages = len(orders[0])
    for s in range(1, stages):
        after = []
        for x, order in zip(chunks, orders):
            size = 1 << len(order[s])
            part = x.shape[0] // size
            total = x[:part]
            for q in range(1, size):
                total = total + send(x[q * part : (q + 1) * part], q * order[s][0], n)
            after.append(total)
        chunks, evals = lax.optimization_barrier((after, evals))
    for s in range(stages - 1, 0, -1):
        chunks = [
            jnp.concatenate(spread_out(x, order[s], n)) for x, order in zip(chunks, orders)
        ]
        chunks = lax.optimization_barrier(chunks)
    return [(x, send(x, first, n)) for x in chunks], evals, masks


def per_device(train_grads, eval_grads, pair_eval, pair_count, n):
    width = train_grads.shape[1]
    nb = width // B
    index = lax.axis_index("dp")
    orders = exchange_orders(n)
    me = jnp.stack([place_of(index, order, n) for order in orders])
    halves = local_gram(me, train_grads, n)
    chunks, evals, masks = all_reduce(
        list(zip(halves[::2], halves[1::2])), eval_grads, orders, n
    )
    blocks = eval_grads.shape[0] * n // EB
    squares = jnp.sum(jnp.square(train_grads.astype(F32)), axis=1)
    scale = lax.rsqrt(squares + EPSILON)[None, :]
    order, count = pair_eval[index], pair_count[index]
    hits = order[:, None] == jnp.arange(blocks, dtype=jnp.int32)[None, :]
    inside = jnp.arange(order.shape[0], dtype=jnp.int32)[:, None] < count
    flags = jnp.any(hits & inside, axis=0).astype(jnp.int32)
    chunks, evals, scale, flags = lax.optimization_barrier((chunks, evals, scale, flags))
    groups = bit_groups(n)
    for group in groups[2:3]:
        evals, masks = gather_stage(evals, masks, group, n)
    hi, lo, end = gram_inverse(me, [x for pair in chunks for x in pair], nb, n)
    evals, end = lax.optimization_barrier((evals, end))
    parts = spread_out(evals, groups[0], n)
    masks = [masks, [m ^ groups[0][0] for m in masks]]
    return scores(
        index[None], flags, parts, masks, eval_grads.shape[0], hi, lo, train_grads, scale, end
    )


def solution(mesh):
    placed = (P(("groups", "dp"), None), P(("groups", "dp"), None), P("groups", None), P("groups"))
    return jax.shard_map(
        functools.partial(per_device, n=mesh.shape["dp"]),
        mesh=mesh,
        in_specs=placed,
        out_specs=P(None, ("groups", "dp")),
        check_vma=False,
    )
```

```python
import functools

import jax
import jax.numpy as jnp
from jax import lax
from jax.experimental import pallas as pl
from jax.experimental.pallas import tpu as pltpu
from jax.sharding import PartitionSpec as P

EB = 256
DAMPING = 0.1
EPSILON = 1e-06
B = 128
F32, BF16 = jnp.float32, jnp.bfloat16
NT = (((1,), (1,)), ((), ()))
NN = (((1,), (0,)), ((), ()))
TN = (((0,), (0,)), ((), ()))
MIB = 1024 * 1024


def dot(a, b, dims):
    return lax.dot_general(a, b, dims, preferred_element_type=F32)


def slab_offset(j, nb):
    return B * (j * nb - j * (j - 1) // 2)


def split3(x):
    hi = x.astype(BF16)
    rest = x - hi.astype(F32)
    mid = rest.astype(BF16)
    lo = (rest - mid.astype(F32)).astype(BF16)
    return hi, mid, lo


def left_parts(x):
    h, m, l = split3(x)
    return jnp.concatenate([h, h, m, m, h, l], axis=1)


def right_parts(x, axis=1):
    h, m, l = split3(x)
    return jnp.concatenate([h, m, h, m, l, h], axis=axis)


def chunk_plan(nb, pieces):
    cut = max(nb // 4, 1)
    plan = []
    for first, last in ((0, cut), (cut, nb)):
        start, stop = slab_offset(first, nb), slab_offset(last, nb)
        rows = -(-(stop - start) // (8 * pieces)) * 8
        plan.append((first, last, start, rows))
    return plan


def gram_kernel(me_ref, t_ref, *refs, nb, pieces):
    width = nb * B
    plan = chunk_plan(nb, pieces)
    outs, packs = refs[: 2 * len(plan)], refs[2 * len(plan) :]

    def chunk_of(j):
        return next(c for c, p in enumerate(plan) if p[0] <= j < p[1])

    for J in range(nb // 2):
        c0 = 2 * B * J
        g = dot(t_ref[:, c0:], t_ref[:, c0 : c0 + 2 * B], TN)
        for h in range(2):
            j = 2 * J + h
            c = chunk_of(j)
            o = slab_offset(j, nb) - plan[c][2]
            packs[c][o : o + width - B * j, :] = g[B * h :, B * h : B * h + B]
    half = pieces // 2
    for c, (first, last, start, rows) in enumerate(plan):
        me = me_ref[c]
        used = slab_offset(last, nb) - start
        if used < pieces * rows:
            packs[c][used:, :] = jnp.zeros((pieces * rows - used, B), F32)
        for q in range(pieces):
            at = pl.multiple_of((me ^ q) * rows, 8)
            out = outs[2 * c + q // half]
            q = q % half
            out[q * rows : (q + 1) * rows, :] = packs[c][pl.ds(at, rows), :]


def local_gram(me, t, pieces):
    nb = t.shape[1] // B
    plan = chunk_plan(nb, pieces)
    halves = [jax.ShapeDtypeStruct((pieces // 2 * p[3], B), F32) for p in plan for _ in range(2)]
    return pl.pallas_call(
        functools.partial(gram_kernel, nb=nb, pieces=pieces),
        out_shape=halves,
        in_specs=[
            pl.BlockSpec(memory_space=pltpu.SMEM),
            pl.BlockSpec(memory_space=pltpu.VMEM),
        ],
        out_specs=[pl.BlockSpec(memory_space=pltpu.VMEM) for _ in halves],
        scratch_shapes=[pltpu.VMEM((pieces * p[3], B), F32) for p in plan],
        compiler_params=pltpu.CompilerParams(vmem_limit_bytes=24 * MIB),
        cost_estimate=pl.CostEstimate(
            flops=t.shape[0] * t.shape[1] * t.shape[1],
            bytes_accessed=t.size * 2 + sum(h.size for h in halves) * 4,
            transcendentals=0,
        ),
        name="local_gram",
    )(me, t)


def reduce_rows(S, R):
    S, R = [list(row) for row in S], list(R)

    def pivot(j, rc):
        s = {k: S[j][k] * rc for k in range(j + 1, 8)}
        row = R[j] * rc
        for i in range(8):
            if i == j:
                continue
            c = S[i][j] if i < j else S[j][i]
            for k in range(max(i, j + 1), 8):
                S[i][k] = S[i][k] - c * s[k]
            R[i] = R[i] - c * row
        for k in s:
            S[j][k] = s[k]
        R[j] = row

    for j in range(0, 8, 2):
        a, b, d = S[j][j], S[j][j + 1], S[j + 1][j + 1]
        rd = 1.0 / (a * d - b * b)
        pivot(j, 1.0 / a)
        pivot(j + 1, a * rd)
    return R


def invert_block(M, spread):
    M = list(M)
    full = (8, B)
    lane = lax.broadcasted_iota(jnp.int32, full, 1)
    sub = lax.broadcasted_iota(jnp.int32, full, 0)
    zero = jnp.zeros(full, F32)
    n, panel = len(M), 8
    for p in range(0, n, panel):
        for b in range(p, p + panel):
            k0 = 8 * b
            columns = lambda V: [
                jnp.broadcast_to(V[:, k0 + k : k0 + k + 1], full) for k in range(8)
            ]
            base = 64 * (b % 2)
            for j, column in enumerate(columns(M[b])):
                spread[base + 8 * j : base + 8 * j + 8, :] = column
            S = [
                [None] * i + [spread[pl.ds(base + 8 * j + i, 8, stride=0), :] for j in range(i, 8)]
                for i in range(8)
            ]
            inside = (lane >= k0) & (lane < k0 + 8)
            R = [
                jnp.where(
                    inside,
                    jnp.where(lane == k0 + i, 1.0, 0.0).astype(F32),
                    jnp.broadcast_to(M[b][i : i + 1, :], full),
                )
                for i in range(8)
            ]
            R = reduce_rows(S, R)
            for q in range(1, panel + 1):
                t = p + (b - p + q) % panel
                if t == b:
                    x = R[0]
                    for i in range(1, 8):
                        x = jnp.where(sub == i, R[i], x)
                else:
                    c = columns(M[t])
                    x, y = jnp.where(inside, 0.0, M[t]) - c[0] * R[0], c[1] * R[1]
                    for k in (2, 4, 6):
                        x, y = x - c[k] * R[k], y + c[k + 1] * R[k + 1]
                    x = x - y
                M[t] = x
        own = range(p, p + panel)
        wide = (lane >= 8 * p) & (lane < 8 * (p + panel))
        C = jnp.concatenate([zero if t in own else jnp.where(wide, M[t], 0.0) for t in range(n)])
        R = jnp.concatenate([M[t] if t in own else zero for t in range(n)])
        U = dot(left_parts(C), right_parts(R, axis=0), NN)
        for t in range(n):
            if t not in own:
                M[t] = jnp.where(wide, 0.0, M[t]) - U[8 * t : 8 * t + 8, :]
    return M


def inverse_kernel(me_ref, *refs, nb, pieces):
    width = nb * B
    plan = chunk_plan(nb, pieces)
    count = len(plan)
    parts, (hi_ref, lo_ref, end_ref) = refs[: 2 * count], refs[2 * count : 2 * count + 3]
    packs = refs[2 * count + 3 : 3 * count + 3]
    A, D, inv, spread, W, WL, CL, CR = refs[3 * count + 3 :]
    half = pieces // 2
    for c, (_, _, _, rows) in enumerate(plan):
        me = me_ref[c]
        for q in range(pieces):
            to = pl.multiple_of((me ^ q) * rows, 8)
            p = q % half
            packs[c][pl.ds(to, rows), :] = parts[2 * c + q // half][p * rows : (p + 1) * rows, :]

    def column(j):
        c = next(c for c, p in enumerate(plan) if p[0] <= j < p[1])
        return packs[c], slab_offset(j, nb) - plan[c][2]

    eye = lax.broadcasted_iota(jnp.int32, (B, B), 0) == lax.broadcasted_iota(
        jnp.int32, (B, B), 1
    )
    diag = jnp.zeros((B, B), F32)
    for j in range(nb):
        pack, o = column(j)
        diag = diag + jnp.where(eye, pack[o : o + B, :], 0.0)
    trace = jnp.sum(jnp.sum(diag, axis=1, keepdims=True), axis=0, keepdims=True)
    scale = jnp.broadcast_to(width / trace, (1, B))
    damp = jnp.where(eye, DAMPING, 0.0).astype(F32)
    for j in range(nb):
        pack, o = column(j)
        A[j, B * j : B * j + B, :] = pack[o : o + B, :] * scale + damp
        if j + 1 < nb:
            A[j, B * j + B :, :] = pack[o + B : o + width - B * j, :] * scale
    MC = 256

    def split_column(k):
        for i in range(nb):
            x = A[k, B * i : B * i + B, :]
            x = jnp.zeros_like(x) if i == k else x
            CL[B * i : B * i + B, :] = left_parts(x)
            CR[B * i : B * i + B, :] = right_parts(x)

    def used(i, j, k):
        return j != k and (i <= k or (j > k and i >= j))

    def eliminate(k):
        pivot = inv[...]
        right = right_parts(pivot, axis=0)
        for i in range(nb):
            w = -pivot if i == k else dot(CL[B * i : B * i + B, :], right, NN)
            W[B * i : B * i + B, :] = w
            WL[B * i : B * i + B, :] = left_parts(w)
        for J in range(nb // 2):
            cols = CR[2 * B * J : 2 * B * (J + 1), :]
            for r in range(0, width, MC):
                blocks = [
                    (r // B + q, 2 * J + h)
                    for h in range(2)
                    for q in range(MC // B)
                    if used(r // B + q, 2 * J + h, k)
                ]
                if not blocks:
                    continue
                u = dot(WL[r : r + MC, :], cols, NT)
                for i, j in blocks:
                    q, h = B * i - r, j - 2 * J
                    x = -u[q : q + B, h * B : h * B + B]
                    if i != k:
                        x = A[j, B * i : B * i + B, :] + x
                    A[j, B * i : B * i + B, :] = x
        A[k] = W[...]

    def invert():
        return jnp.concatenate(
            invert_block([D[8 * t : 8 * t + 8, :] for t in range(B // 8)], spread)
        )

    def next_pivot(k):
        at = slice(B * k, B * k + B)
        w = dot(CL[at, :], right_parts(inv[...], axis=0), NN)
        D[...] = A[k, at, :] - dot(left_parts(w), CR[at, :], NT)

    D[...] = A[0, :B, :]
    split_column(0)
    inv[...] = invert()
    for k in range(nb - 1):
        next_pivot(k + 1)
        eliminate(k)
        split_column(k + 1)
        inv[...] = invert()
    eliminate(nb - 1)
    end_ref[...] = jnp.zeros_like(end_ref)
    for j in range(nb):
        x = -A[j]
        hi = x.astype(BF16)
        hi_ref[:, B * j : B * j + B] = hi
        lo_ref[:, B * j : B * j + B] = (x - hi.astype(F32)).astype(BF16)


def gram_inverse(me, parts, nb, pieces):
    width = nb * B
    out = jax.ShapeDtypeStruct((width, width), BF16)
    return pl.pallas_call(
        functools.partial(inverse_kernel, nb=nb, pieces=pieces),
        out_shape=(out, out, jax.ShapeDtypeStruct((8, B), F32)),
        in_specs=[pl.BlockSpec(memory_space=pltpu.SMEM)]
        + [pl.BlockSpec(memory_space=pltpu.VMEM) for _ in parts],
        out_specs=(pl.BlockSpec(memory_space=pltpu.VMEM),) * 3,
        scratch_shapes=[pltpu.VMEM((pieces * p[3], B), F32) for p in chunk_plan(nb, pieces)]
        + [
            pltpu.VMEM((nb, width, B), F32),
            pltpu.VMEM((B, B), F32),
            pltpu.VMEM((B, B), F32),
            pltpu.VMEM((B, B), F32),
            pltpu.VMEM((width, B), F32),
            pltpu.VMEM((width, 6 * B), BF16),
            pltpu.VMEM((width, 6 * B), BF16),
            pltpu.VMEM((width, 6 * B), BF16),
        ],
        compiler_params=pltpu.CompilerParams(vmem_limit_bytes=32 * MIB),
        cost_estimate=pl.CostEstimate(
            flops=24 * width**3, bytes_accessed=width * width * 8, transcendentals=0
        ),
        name="gram_inverse",
    )(me, *parts)


def score_kernel(me_ref, flag_ref, hi_ref, lo_ref, t_ref, scale_ref, end_ref, *refs, rows, masks):
    parts, out_ref, evals = refs[:-2], refs[-2], refs[-1]
    e = pl.program_id(0)

    @pl.when(e == 0)
    def _():
        for part, held in zip(parts, masks):
            for q, mask in enumerate(held):
                to = pl.multiple_of((me_ref[0] ^ mask) * rows, 16)
                evals[pl.ds(to, rows), :] = part[q * rows : (q + 1) * rows, :]

    @pl.when(flag_ref[e] > 0)
    def _():
        block = evals[pl.ds(pl.multiple_of(e * EB, EB), EB), :]
        pre = (dot(block, hi_ref[...], NN) + dot(block, lo_ref[...], NN)).astype(BF16)
        score = dot(pre, t_ref[...], NT)
        out_ref[pl.ds(e, 1), :] = jnp.max(score, axis=0, keepdims=True) * scale_ref[...]

    @pl.when(flag_ref[e] <= 0)
    def _():
        out_ref[pl.ds(e, 1), :] = jnp.zeros((1, out_ref.shape[1]), F32)


def scores(index, flags, parts, masks, rows, hi, lo, t, scale, end):
    total = sum(p.shape[0] for p in parts)
    blocks = total // EB
    width = t.shape[1]
    whole = lambda shape: pl.BlockSpec(shape, lambda e: (0, 0))
    smem = pl.BlockSpec(memory_space=pltpu.SMEM)
    operands = (hi, lo, t, scale, end) + tuple(parts)
    return pl.pallas_call(
        functools.partial(score_kernel, rows=rows, masks=masks),
        grid=(blocks,),
        out_shape=jax.ShapeDtypeStruct((blocks, t.shape[0]), F32),
        in_specs=[smem, smem] + [whole(x.shape) for x in operands],
        out_specs=whole((blocks, t.shape[0])),
        scratch_shapes=[pltpu.VMEM((total, width), BF16)],
        compiler_params=pltpu.CompilerParams(vmem_limit_bytes=20 * MIB + 8 * total * width),
        cost_estimate=pl.CostEstimate(
            flops=6 * total * width * width,
            bytes_accessed=total * width * 2 + width * width * 6,
            transcendentals=0,
        ),
        name="scores",
    )(index, flags, *operands)


def bit_groups(n):
    bits = [1 << s for s in range(n.bit_length() - 1)]
    groups = [[b] for b in bits[:2]]
    rest = bits[2:]
    while rest:
        groups.append(rest[:2])
        rest = rest[2:]
    return groups


def send(x, mask, n):
    return lax.ppermute(x, "dp", [(i, i ^ mask) for i in range(n)])


def exchange_orders(n):
    groups = bit_groups(n)
    return [groups[:1] + groups[:0:-1], groups]


def place_of(index, order, n):
    place, step = 0, n
    for group in order:
        size = 1 << len(group)
        step //= size
        place = place + (index // group[0]) % size * step
    return place


def spread_out(x, group, n):
    return [x] + [send(x, q * group[0], n) for q in range(1, 1 << len(group))]


def gather_stage(x, masks, group, n):
    steps = [q * group[0] for q in range(1 << len(group))]
    return jnp.concatenate(spread_out(x, group, n)), [m ^ step for step in steps for m in masks]


def all_reduce(chunks, evals, orders, n):
    first = orders[0][0][0]
    chunks = [keep + send(other, first, n) for keep, other in chunks]
    groups, masks = bit_groups(n), [0]
    for group in groups[1:2] + groups[3:]:
        evals, masks = gather_stage(evals, masks, group, n)
    stages = len(orders[0])
    for s in range(1, stages):
        after = []
        for x, order in zip(chunks, orders):
            size = 1 << len(order[s])
            part = x.shape[0] // size
            total = x[:part]
            for q in range(1, size):
                total = total + send(x[q * part : (q + 1) * part], q * order[s][0], n)
            after.append(total)
        chunks, evals = lax.optimization_barrier((after, evals))
    for s in range(stages - 1, 0, -1):
        chunks = [
            jnp.concatenate(spread_out(x, order[s], n)) for x, order in zip(chunks, orders)
        ]
        chunks = lax.optimization_barrier(chunks)
    return [(x, send(x, first, n)) for x in chunks], evals, masks


def per_device(train_grads, eval_grads, pair_eval, pair_count, n):
    width = train_grads.shape[1]
    nb = width // B
    index = lax.axis_index("dp")
    orders = exchange_orders(n)
    me = jnp.stack([place_of(index, order, n) for order in orders])
    halves = local_gram(me, train_grads, n)
    chunks, evals, masks = all_reduce(
        list(zip(halves[::2], halves[1::2])), eval_grads, orders, n
    )
    blocks = eval_grads.shape[0] * n // EB
    squares = jnp.sum(jnp.square(train_grads.astype(F32)), axis=1)
    scale = lax.rsqrt(squares + EPSILON)[None, :]
    order, count = pair_eval[index], pair_count[index]
    hits = order[:, None] == jnp.arange(blocks, dtype=jnp.int32)[None, :]
    inside = jnp.arange(order.shape[0], dtype=jnp.int32)[:, None] < count
    flags = jnp.any(hits & inside, axis=0).astype(jnp.int32)
    chunks, evals, scale, flags = lax.optimization_barrier((chunks, evals, scale, flags))
    groups = bit_groups(n)
    for group in groups[2:3]:
        evals, masks = gather_stage(evals, masks, group, n)
    hi, lo, end = gram_inverse(me, [x for pair in chunks for x in pair], nb, n)
    evals, end = lax.optimization_barrier((evals, end))
    parts = spread_out(evals, groups[0], n)
    masks = [masks, [m ^ groups[0][0] for m in masks]]
    return scores(
        index[None], flags, parts, masks, eval_grads.shape[0], hi, lo, train_grads, scale, end
    )


def solution(mesh):
    placed = (P(("groups", "dp"), None), P(("groups", "dp"), None), P("groups", None), P("groups"))
    return jax.shard_map(
        functools.partial(per_device, n=mesh.shape["dp"]),
        mesh=mesh,
        in_specs=placed,
        out_specs=P(None, ("groups", "dp")),
        check_vma=False,
    )
```

```python
import functools

import jax
import jax.numpy as jnp
from jax import lax
from jax.experimental import pallas as pl
from jax.experimental.pallas import tpu as pltpu
from jax.sharding import PartitionSpec as P

EB = 256
DAMPING = 0.1
EPSILON = 1e-06
B = 128
F32, BF16 = jnp.float32, jnp.bfloat16
NT = (((1,), (1,)), ((), ()))
NN = (((1,), (0,)), ((), ()))
TN = (((0,), (0,)), ((), ()))
MIB = 1024 * 1024


def dot(a, b, dims):
    return lax.dot_general(a, b, dims, preferred_element_type=F32)


def slab_offset(j, nb):
    return B * (j * nb - j * (j - 1) // 2)


def split3(x):
    hi = x.astype(BF16)
    rest = x - hi.astype(F32)
    mid = rest.astype(BF16)
    lo = (rest - mid.astype(F32)).astype(BF16)
    return hi, mid, lo


def left_parts(x):
    h, m, l = split3(x)
    return jnp.concatenate([h, h, m, m, h, l], axis=1)


def right_parts(x, axis=1):
    h, m, l = split3(x)
    return jnp.concatenate([h, m, h, m, l, h], axis=axis)


def chunk_plan(nb, pieces):
    cut = max(nb // 4, 1)
    plan = []
    for first, last in ((0, cut), (cut, nb)):
        start, stop = slab_offset(first, nb), slab_offset(last, nb)
        rows = -(-(stop - start) // (8 * pieces)) * 8
        plan.append((first, last, start, rows))
    return plan


def gram_kernel(me_ref, t_ref, *refs, nb, pieces):
    width = nb * B
    plan = chunk_plan(nb, pieces)
    outs, packs = refs[: 2 * len(plan)], refs[2 * len(plan) :]

    def chunk_of(j):
        return next(c for c, p in enumerate(plan) if p[0] <= j < p[1])

    for J in range(nb // 2):
        c0 = 2 * B * J
        g = dot(t_ref[:, c0:], t_ref[:, c0 : c0 + 2 * B], TN)
        for h in range(2):
            j = 2 * J + h
            c = chunk_of(j)
            o = slab_offset(j, nb) - plan[c][2]
            packs[c][o : o + width - B * j, :] = g[B * h :, B * h : B * h + B]
    half = pieces // 2
    for c, (first, last, start, rows) in enumerate(plan):
        me = me_ref[c]
        used = slab_offset(last, nb) - start
        if used < pieces * rows:
            packs[c][used:, :] = jnp.zeros((pieces * rows - used, B), F32)
        for q in range(pieces):
            at = pl.multiple_of((me ^ q) * rows, 8)
            out = outs[2 * c + q // half]
            q = q % half
            out[q * rows : (q + 1) * rows, :] = packs[c][pl.ds(at, rows), :]


def local_gram(me, t, pieces):
    nb = t.shape[1] // B
    plan = chunk_plan(nb, pieces)
    halves = [jax.ShapeDtypeStruct((pieces // 2 * p[3], B), F32) for p in plan for _ in range(2)]
    return pl.pallas_call(
        functools.partial(gram_kernel, nb=nb, pieces=pieces),
        out_shape=halves,
        in_specs=[
            pl.BlockSpec(memory_space=pltpu.SMEM),
            pl.BlockSpec(memory_space=pltpu.VMEM),
        ],
        out_specs=[pl.BlockSpec(memory_space=pltpu.VMEM) for _ in halves],
        scratch_shapes=[pltpu.VMEM((pieces * p[3], B), F32) for p in plan],
        compiler_params=pltpu.CompilerParams(vmem_limit_bytes=24 * MIB),
        cost_estimate=pl.CostEstimate(
            flops=t.shape[0] * t.shape[1] * t.shape[1],
            bytes_accessed=t.size * 2 + sum(h.size for h in halves) * 4,
            transcendentals=0,
        ),
        name="local_gram",
    )(me, t)


def reduce_rows(S, R):
    S, R = [list(row) for row in S], list(R)

    def pivot(j, rc):
        s = {k: S[j][k] * rc for k in range(j + 1, 8)}
        row = R[j] * rc
        for i in range(8):
            if i == j:
                continue
            c = S[i][j] if i < j else S[j][i]
            for k in range(max(i, j + 1), 8):
                S[i][k] = S[i][k] - c * s[k]
            R[i] = R[i] - c * row
        for k in s:
            S[j][k] = s[k]
        R[j] = row

    for j in range(0, 8, 2):
        a, b, d = S[j][j], S[j][j + 1], S[j + 1][j + 1]
        rd = 1.0 / (a * d - b * b)
        pivot(j, 1.0 / a)
        pivot(j + 1, a * rd)
    return R


def invert_block(M, spread):
    M = list(M)
    full = (8, B)
    lane = lax.broadcasted_iota(jnp.int32, full, 1)
    sub = lax.broadcasted_iota(jnp.int32, full, 0)
    zero = jnp.zeros(full, F32)
    n, panel = len(M), 8
    for p in range(0, n, panel):
        for b in range(p, p + panel):
            k0 = 8 * b
            columns = lambda V: [
                jnp.broadcast_to(V[:, k0 + k : k0 + k + 1], full) for k in range(8)
            ]
            base = 64 * (b % 2)
            for j, column in enumerate(columns(M[b])):
                spread[base + 8 * j : base + 8 * j + 8, :] = column
            S = [
                [None] * i + [spread[pl.ds(base + 8 * j + i, 8, stride=0), :] for j in range(i, 8)]
                for i in range(8)
            ]
            inside = (lane >= k0) & (lane < k0 + 8)
            R = [
                jnp.where(
                    inside,
                    jnp.where(lane == k0 + i, 1.0, 0.0).astype(F32),
                    jnp.broadcast_to(M[b][i : i + 1, :], full),
                )
                for i in range(8)
            ]
            R = reduce_rows(S, R)
            for q in range(1, panel + 1):
                t = p + (b - p + q) % panel
                if t == b:
                    x = R[0]
                    for i in range(1, 8):
                        x = jnp.where(sub == i, R[i], x)
                else:
                    c = columns(M[t])
                    x, y = jnp.where(inside, 0.0, M[t]) - c[0] * R[0], c[1] * R[1]
                    for k in (2, 4, 6):
                        x, y = x - c[k] * R[k], y + c[k + 1] * R[k + 1]
                    x = x - y
                M[t] = x
        own = range(p, p + panel)
        wide = (lane >= 8 * p) & (lane < 8 * (p + panel))
        others = [t for t in range(n) if t not in own]
        C = jnp.concatenate([jnp.where(wide, M[t], 0.0) for t in others])
        R = jnp.concatenate([M[t] if t in own else zero for t in range(n)])
        U = dot(left_parts(C), right_parts(R, axis=0), NN)
        for r, t in enumerate(others):
            M[t] = jnp.where(wide, 0.0, M[t]) - U[8 * r : 8 * r + 8, :]
    return M


def inverse_kernel(me_ref, *refs, nb, pieces):
    width = nb * B
    plan = chunk_plan(nb, pieces)
    count = len(plan)
    parts, (hi_ref, lo_ref, end_ref) = refs[: 2 * count], refs[2 * count : 2 * count + 3]
    packs = refs[2 * count + 3 : 3 * count + 3]
    A, D, inv, spread, W, WL, CL, CR = refs[3 * count + 3 :]
    half = pieces // 2
    for c, (_, _, _, rows) in enumerate(plan):
        me = me_ref[c]
        for q in range(pieces):
            to = pl.multiple_of((me ^ q) * rows, 8)
            p = q % half
            packs[c][pl.ds(to, rows), :] = parts[2 * c + q // half][p * rows : (p + 1) * rows, :]

    def column(j):
        c = next(c for c, p in enumerate(plan) if p[0] <= j < p[1])
        return packs[c], slab_offset(j, nb) - plan[c][2]

    eye = lax.broadcasted_iota(jnp.int32, (B, B), 0) == lax.broadcasted_iota(
        jnp.int32, (B, B), 1
    )
    diag = jnp.zeros((B, B), F32)
    for j in range(nb):
        pack, o = column(j)
        diag = diag + jnp.where(eye, pack[o : o + B, :], 0.0)
    trace = jnp.sum(jnp.sum(diag, axis=1, keepdims=True), axis=0, keepdims=True)
    scale = jnp.broadcast_to(width / trace, (1, B))
    damp = jnp.where(eye, DAMPING, 0.0).astype(F32)
    for j in range(nb):
        pack, o = column(j)
        A[j, B * j : B * j + B, :] = pack[o : o + B, :] * scale + damp
        if j + 1 < nb:
            A[j, B * j + B :, :] = pack[o + B : o + width - B * j, :] * scale
    MC = 256

    def split_column(k):
        for i in range(nb):
            x = A[k, B * i : B * i + B, :]
            x = jnp.zeros_like(x) if i == k else x
            CL[B * i : B * i + B, :] = left_parts(x)
            CR[B * i : B * i + B, :] = right_parts(x)

    def used(i, j, k):
        return j != k and (i <= k or (j > k and i >= j))

    def eliminate(k):
        pivot = inv[...]
        right = right_parts(pivot, axis=0)
        for i in range(nb):
            w = -pivot if i == k else dot(CL[B * i : B * i + B, :], right, NN)
            W[B * i : B * i + B, :] = w
            WL[B * i : B * i + B, :] = left_parts(w)
        for J in range(nb // 2):
            cols = CR[2 * B * J : 2 * B * (J + 1), :]
            for r in range(0, width, MC):
                blocks = [
                    (r // B + q, 2 * J + h)
                    for h in range(2)
                    for q in range(MC // B)
                    if used(r // B + q, 2 * J + h, k)
                ]
                if not blocks:
                    continue
                u = dot(WL[r : r + MC, :], cols, NT)
                for i, j in blocks:
                    q, h = B * i - r, j - 2 * J
                    x = -u[q : q + B, h * B : h * B + B]
                    if i != k:
                        x = A[j, B * i : B * i + B, :] + x
                    A[j, B * i : B * i + B, :] = x
        A[k] = W[...]

    def invert():
        return jnp.concatenate(
            invert_block([D[8 * t : 8 * t + 8, :] for t in range(B // 8)], spread)
        )

    def next_pivot(k):
        at = slice(B * k, B * k + B)
        w = dot(CL[at, :], right_parts(inv[...], axis=0), NN)
        D[...] = A[k, at, :] - dot(left_parts(w), CR[at, :], NT)

    D[...] = A[0, :B, :]
    split_column(0)
    inv[...] = invert()
    for k in range(nb - 1):
        next_pivot(k + 1)
        eliminate(k)
        split_column(k + 1)
        inv[...] = invert()
    eliminate(nb - 1)
    end_ref[...] = jnp.zeros_like(end_ref)
    for j in range(nb):
        x = -A[j]
        hi = x.astype(BF16)
        hi_ref[:, B * j : B * j + B] = hi
        lo_ref[:, B * j : B * j + B] = (x - hi.astype(F32)).astype(BF16)


def gram_inverse(me, parts, nb, pieces):
    width = nb * B
    out = jax.ShapeDtypeStruct((width, width), BF16)
    return pl.pallas_call(
        functools.partial(inverse_kernel, nb=nb, pieces=pieces),
        out_shape=(out, out, jax.ShapeDtypeStruct((8, B), F32)),
        in_specs=[pl.BlockSpec(memory_space=pltpu.SMEM)]
        + [pl.BlockSpec(memory_space=pltpu.VMEM) for _ in parts],
        out_specs=(pl.BlockSpec(memory_space=pltpu.VMEM),) * 3,
        scratch_shapes=[pltpu.VMEM((pieces * p[3], B), F32) for p in chunk_plan(nb, pieces)]
        + [
            pltpu.VMEM((nb, width, B), F32),
            pltpu.VMEM((B, B), F32),
            pltpu.VMEM((B, B), F32),
            pltpu.VMEM((B, B), F32),
            pltpu.VMEM((width, B), F32),
            pltpu.VMEM((width, 6 * B), BF16),
            pltpu.VMEM((width, 6 * B), BF16),
            pltpu.VMEM((width, 6 * B), BF16),
        ],
        compiler_params=pltpu.CompilerParams(vmem_limit_bytes=32 * MIB),
        cost_estimate=pl.CostEstimate(
            flops=24 * width**3, bytes_accessed=width * width * 8, transcendentals=0
        ),
        name="gram_inverse",
    )(me, *parts)


def score_kernel(me_ref, hi_ref, lo_ref, t_ref, part_ref, *refs, rows, masks):
    finish, out_ref, evals = refs[:-2], refs[-2], refs[-1]
    for q, mask in enumerate(masks):
        chip = lax.shift_right_logical(me_ref[0] ^ mask, 1)
        to = pl.multiple_of(chip * rows, 16)
        evals[pl.ds(to, rows), :] = part_ref[q * rows : (q + 1) * rows, :]
    span = EB // 2
    blocks = part_ref.shape[0] // span
    at_once = min(4, blocks)
    for c in range(0, blocks, at_once):
        some = evals[c * span : (c + at_once) * span, :]
        pre = (dot(some, hi_ref[...], NN) + dot(some, lo_ref[...], NN)).astype(BF16)
        score = dot(pre, t_ref[...], NT)
        for e in range(at_once):
            top = jnp.max(score[e * span : (e + 1) * span, :], axis=0, keepdims=True)
            row = slice(c + e, c + e + 1)
            if finish:
                flag_ref, scale_ref, prior_ref, _ = finish
                top = jnp.maximum(top, prior_ref[row, :]) * scale_ref[...]
                top = jnp.where(flag_ref[c + e] > 0, top, jnp.zeros_like(top))
            out_ref[row, :] = top


def scores(index, part, masks, rows, hi, lo, t, finish=()):
    blocks = part.shape[0] // (EB // 2)
    width = t.shape[1]
    smem = pl.BlockSpec(memory_space=pltpu.SMEM)
    vmem = pl.BlockSpec(memory_space=pltpu.VMEM)
    return pl.pallas_call(
        functools.partial(score_kernel, rows=rows, masks=masks),
        out_shape=jax.ShapeDtypeStruct((blocks, t.shape[0]), F32),
        in_specs=[smem] + [vmem] * 4 + ([smem] + [vmem] * 3 if finish else []),
        out_specs=vmem,
        scratch_shapes=[pltpu.VMEM(part.shape, BF16)],
        compiler_params=pltpu.CompilerParams(vmem_limit_bytes=20 * MIB + 8 * part.size),
        cost_estimate=pl.CostEstimate(
            flops=6 * part.size * width,
            bytes_accessed=part.size * 2 + width * width * 6,
            transcendentals=0,
        ),
        name="scores_joined" if finish else "scores_own",
    )(index, hi, lo, t, part, *finish)


def bit_groups(n):
    bits = [1 << s for s in range(n.bit_length() - 1)]
    groups = [[b] for b in bits[:2]]
    rest = bits[2:]
    while rest:
        groups.append(rest[:2])
        rest = rest[2:]
    return groups


def send(x, mask, n):
    return lax.ppermute(x, "dp", [(i, i ^ mask) for i in range(n)])


def exchange_orders(n):
    groups = bit_groups(n)
    return [groups[:1] + groups[:0:-1], groups]


def place_of(index, order, n):
    place, step = 0, n
    for group in order:
        size = 1 << len(group)
        step //= size
        place = place + (index // group[0]) % size * step
    return place


def spread_out(x, group, n):
    return [x] + [send(x, q * group[0], n) for q in range(1, 1 << len(group))]


def gather_stage(x, masks, group, n):
    steps = [q * group[0] for q in range(1 << len(group))]
    return jnp.concatenate(spread_out(x, group, n)), [m ^ step for step in steps for m in masks]


def all_reduce(chunks, evals, orders, n):
    first = orders[0][0][0]
    chunks = [keep + send(other, first, n) for keep, other in chunks]
    groups, masks = bit_groups(n), [0]
    for group in groups[1:2] + groups[3:]:
        evals, masks = gather_stage(evals, masks, group, n)
    stages = len(orders[0])
    for s in range(1, stages):
        after = []
        for x, order in zip(chunks, orders):
            size = 1 << len(order[s])
            part = x.shape[0] // size
            total = x[:part]
            for q in range(1, size):
                total = total + send(x[q * part : (q + 1) * part], q * order[s][0], n)
            after.append(total)
        chunks, evals = lax.optimization_barrier((after, evals))
    for s in range(stages - 1, 0, -1):
        chunks = [
            jnp.concatenate(spread_out(x, order[s], n)) for x, order in zip(chunks, orders)
        ]
        chunks = lax.optimization_barrier(chunks)
    return [(x, send(x, first, n)) for x in chunks], evals, masks


def per_device(train_grads, eval_grads, pair_eval, pair_count, n):
    width = train_grads.shape[1]
    nb = width // B
    index = lax.axis_index("dp")
    orders = exchange_orders(n)
    me = jnp.stack([place_of(index, order, n) for order in orders])
    halves = local_gram(me, train_grads, n)
    chunks, evals, masks = all_reduce(
        list(zip(halves[::2], halves[1::2])), eval_grads, orders, n
    )
    blocks = eval_grads.shape[0] * n // EB
    squares = jnp.sum(jnp.square(train_grads.astype(F32)), axis=1)
    scale = lax.rsqrt(squares + EPSILON)[None, :]
    order, count = pair_eval[index], pair_count[index]
    hits = order[:, None] == jnp.arange(blocks, dtype=jnp.int32)[None, :]
    inside = jnp.arange(order.shape[0], dtype=jnp.int32)[:, None] < count
    flags = jnp.any(hits & inside, axis=0).astype(jnp.int32)
    chunks, evals, scale, flags = lax.optimization_barrier((chunks, evals, scale, flags))
    groups = bit_groups(n)
    for group in groups[2:3]:
        evals, masks = gather_stage(evals, masks, group, n)
    hi, lo, end = gram_inverse(me, [x for pair in chunks for x in pair], nb, n)
    evals, end = lax.optimization_barrier((evals, end))
    other = send(evals, groups[0][0], n)
    rows, core = eval_grads.shape[0], groups[0][0]
    own = scores(index[None], evals, masks, rows, hi, lo, train_grads)
    masks = [m ^ core for m in masks]
    finish = (flags, scale, own, end)
    return scores(index[None], other, masks, rows, hi, lo, train_grads, finish)


def solution(mesh):
    placed = (P(("groups", "dp"), None), P(("groups", "dp"), None), P("groups", None), P("groups"))
    return jax.shard_map(
        functools.partial(per_device, n=mesh.shape["dp"]),
        mesh=mesh,
        in_specs=placed,
        out_specs=P(None, ("groups", "dp")),
        check_vma=False,
    )
```

```python
import functools

import jax
import jax.numpy as jnp
from jax import lax
from jax.experimental import pallas as pl
from jax.experimental.pallas import tpu as pltpu
from jax.sharding import PartitionSpec as P

EB = 256
DAMPING = 0.1
EPSILON = 1e-06
B = 128
F32, BF16 = jnp.float32, jnp.bfloat16
NT = (((1,), (1,)), ((), ()))
NN = (((1,), (0,)), ((), ()))
TN = (((0,), (0,)), ((), ()))
MIB = 1024 * 1024


def dot(a, b, dims):
    return lax.dot_general(a, b, dims, preferred_element_type=F32)


def slab_offset(j, nb):
    return B * (j * nb - j * (j - 1) // 2)


def split3(x):
    hi = x.astype(BF16)
    rest = x - hi.astype(F32)
    mid = rest.astype(BF16)
    lo = (rest - mid.astype(F32)).astype(BF16)
    return hi, mid, lo


def left_parts(x):
    h, m, l = split3(x)
    return jnp.concatenate([h, h, m, m, h, l], axis=1)


def right_parts(x, axis=1):
    h, m, l = split3(x)
    return jnp.concatenate([h, m, h, m, l, h], axis=axis)


def chunk_plan(nb, pieces):
    cut = max(nb // 4, 1)
    plan = []
    for first, last in ((0, cut), (cut, nb)):
        start, stop = slab_offset(first, nb), slab_offset(last, nb)
        rows = -(-(stop - start) // (8 * pieces)) * 8
        plan.append((first, last, start, rows))
    return plan


def gram_kernel(me_ref, t_ref, *refs, nb, pieces):
    width = nb * B
    plan = chunk_plan(nb, pieces)
    outs, packs = refs[: 2 * len(plan)], refs[2 * len(plan) :]

    def chunk_of(j):
        return next(c for c, p in enumerate(plan) if p[0] <= j < p[1])

    for J in range(nb // 2):
        c0 = 2 * B * J
        g = dot(t_ref[:, c0:], t_ref[:, c0 : c0 + 2 * B], TN)
        for h in range(2):
            j = 2 * J + h
            c = chunk_of(j)
            o = slab_offset(j, nb) - plan[c][2]
            packs[c][o : o + width - B * j, :] = g[B * h :, B * h : B * h + B]
    half = pieces // 2
    for c, (first, last, start, rows) in enumerate(plan):
        me = me_ref[c]
        used = slab_offset(last, nb) - start
        if used < pieces * rows:
            packs[c][used:, :] = jnp.zeros((pieces * rows - used, B), F32)
        for q in range(pieces):
            at = pl.multiple_of((me ^ q) * rows, 8)
            out = outs[2 * c + q // half]
            q = q % half
            out[q * rows : (q + 1) * rows, :] = packs[c][pl.ds(at, rows), :]


def local_gram(me, t, pieces):
    nb = t.shape[1] // B
    plan = chunk_plan(nb, pieces)
    halves = [jax.ShapeDtypeStruct((pieces // 2 * p[3], B), F32) for p in plan for _ in range(2)]
    return pl.pallas_call(
        functools.partial(gram_kernel, nb=nb, pieces=pieces),
        out_shape=halves,
        in_specs=[
            pl.BlockSpec(memory_space=pltpu.SMEM),
            pl.BlockSpec(memory_space=pltpu.VMEM),
        ],
        out_specs=[pl.BlockSpec(memory_space=pltpu.VMEM) for _ in halves],
        scratch_shapes=[pltpu.VMEM((pieces * p[3], B), F32) for p in plan],
        compiler_params=pltpu.CompilerParams(vmem_limit_bytes=24 * MIB),
        cost_estimate=pl.CostEstimate(
            flops=t.shape[0] * t.shape[1] * t.shape[1],
            bytes_accessed=t.size * 2 + sum(h.size for h in halves) * 4,
            transcendentals=0,
        ),
        name="local_gram",
    )(me, t)


def reduce_rows(S, R):
    S, R = [list(row) for row in S], list(R)

    def pivot(j, rc):
        s = {k: S[j][k] * rc for k in range(j + 1, 8)}
        row = R[j] * rc
        for i in range(8):
            if i == j:
                continue
            c = S[i][j] if i < j else S[j][i]
            for k in range(max(i, j + 1), 8):
                S[i][k] = S[i][k] - c * s[k]
            R[i] = R[i] - c * row
        for k in s:
            S[j][k] = s[k]
        R[j] = row

    for j in range(0, 8, 2):
        a, b, d = S[j][j], S[j][j + 1], S[j + 1][j + 1]
        rd = 1.0 / (a * d - b * b)
        pivot(j, 1.0 / a)
        pivot(j + 1, a * rd)
    return R


def invert_block(M, spread):
    M = list(M)
    full = (8, B)
    lane = lax.broadcasted_iota(jnp.int32, full, 1)
    sub = lax.broadcasted_iota(jnp.int32, full, 0)
    zero = jnp.zeros(full, F32)
    n, panel = len(M), 8
    for p in range(0, n, panel):
        for b in range(p, p + panel):
            k0 = 8 * b
            columns = lambda V: [
                jnp.broadcast_to(V[:, k0 + k : k0 + k + 1], full) for k in range(8)
            ]
            base = 64 * (b % 2)
            for j, column in enumerate(columns(M[b])):
                spread[base + 8 * j : base + 8 * j + 8, :] = column
            S = [
                [None] * i + [spread[pl.ds(base + 8 * j + i, 8, stride=0), :] for j in range(i, 8)]
                for i in range(8)
            ]
            inside = (lane >= k0) & (lane < k0 + 8)
            R = [
                jnp.where(
                    inside,
                    jnp.where(lane == k0 + i, 1.0, 0.0).astype(F32),
                    jnp.broadcast_to(M[b][i : i + 1, :], full),
                )
                for i in range(8)
            ]
            R = reduce_rows(S, R)
            for q in range(1, panel + 1):
                t = p + (b - p + q) % panel
                if t == b:
                    x = R[0]
                    for i in range(1, 8):
                        x = jnp.where(sub == i, R[i], x)
                else:
                    c = columns(M[t])
                    x, y = jnp.where(inside, 0.0, M[t]) - c[0] * R[0], c[1] * R[1]
                    for k in (2, 4, 6):
                        x, y = x - c[k] * R[k], y + c[k + 1] * R[k + 1]
                    x = x - y
                M[t] = x
        own = range(p, p + panel)
        wide = (lane >= 8 * p) & (lane < 8 * (p + panel))
        C = jnp.concatenate([zero if t in own else jnp.where(wide, M[t], 0.0) for t in range(n)])
        R = jnp.concatenate([M[t] if t in own else zero for t in range(n)])
        U = dot(left_parts(C), right_parts(R, axis=0), NN)
        for t in range(n):
            if t not in own:
                M[t] = jnp.where(wide, 0.0, M[t]) - U[8 * t : 8 * t + 8, :]
    return M


def inverse_kernel(me_ref, *refs, nb, pieces):
    width = nb * B
    plan = chunk_plan(nb, pieces)
    count = len(plan)
    parts, (hi_ref, lo_ref, end_ref) = refs[: 2 * count], refs[2 * count : 2 * count + 3]
    packs = refs[2 * count + 3 : 3 * count + 3]
    A, D, inv, spread, W, WL, CL, CR = refs[3 * count + 3 :]
    half = pieces // 2
    for c, (_, _, _, rows) in enumerate(plan):
        me = me_ref[c]
        for q in range(pieces):
            to = pl.multiple_of((me ^ q) * rows, 8)
            p = q % half
            packs[c][pl.ds(to, rows), :] = parts[2 * c + q // half][p * rows : (p + 1) * rows, :]

    def column(j):
        c = next(c for c, p in enumerate(plan) if p[0] <= j < p[1])
        return packs[c], slab_offset(j, nb) - plan[c][2]

    eye = lax.broadcasted_iota(jnp.int32, (B, B), 0) == lax.broadcasted_iota(
        jnp.int32, (B, B), 1
    )
    diag = jnp.zeros((B, B), F32)
    for j in range(nb):
        pack, o = column(j)
        diag = diag + jnp.where(eye, pack[o : o + B, :], 0.0)
    trace = jnp.sum(jnp.sum(diag, axis=1, keepdims=True), axis=0, keepdims=True)
    scale = jnp.broadcast_to(width / trace, (1, B))
    damp = jnp.where(eye, DAMPING, 0.0).astype(F32)
    for j in range(nb):
        pack, o = column(j)
        A[j, B * j : B * j + B, :] = pack[o : o + B, :] * scale + damp
        if j + 1 < nb:
            A[j, B * j + B :, :] = pack[o + B : o + width - B * j, :] * scale
    MC = 256

    def split_column(k):
        for i in range(nb):
            x = A[k, B * i : B * i + B, :]
            x = jnp.zeros_like(x) if i == k else x
            CL[B * i : B * i + B, :] = left_parts(x)
            CR[B * i : B * i + B, :] = right_parts(x)

    def used(i, j, k):
        return j != k and (i <= k or (j > k and i >= j))

    def put(i, j, x):
        hi = (-x).astype(BF16)
        at = (slice(B * i, B * i + B), slice(B * j, B * j + B))
        hi_ref[at] = hi
        lo_ref[at] = (-x - hi.astype(F32)).astype(BF16)

    def eliminate(k):
        pivot = inv[...]
        right = right_parts(pivot, axis=0)
        for i in range(nb):
            w = -pivot if i == k else dot(CL[B * i : B * i + B, :], right, NN)
            W[B * i : B * i + B, :] = w
            WL[B * i : B * i + B, :] = left_parts(w)
        for J in range(nb // 2):
            cols = CR[2 * B * J : 2 * B * (J + 1), :]
            for r in range(0, width, MC):
                blocks = [
                    (r // B + q, 2 * J + h)
                    for h in range(2)
                    for q in range(MC // B)
                    if used(r // B + q, 2 * J + h, k)
                ]
                if not blocks:
                    continue
                u = dot(WL[r : r + MC, :], cols, NT)
                for i, j in blocks:
                    q, h = B * i - r, j - 2 * J
                    x = -u[q : q + B, h * B : h * B + B]
                    if i != k:
                        x = A[j, B * i : B * i + B, :] + x
                    if k == nb - 1:
                        put(i, j, x)
                    else:
                        A[j, B * i : B * i + B, :] = x
        if k == nb - 1:
            for i in range(nb):
                put(i, k, W[B * i : B * i + B, :])
        else:
            A[k] = W[...]

    def invert():
        return jnp.concatenate(
            invert_block([D[8 * t : 8 * t + 8, :] for t in range(B // 8)], spread)
        )

    def next_pivot(k):
        at = slice(B * k, B * k + B)
        w = dot(CL[at, :], right_parts(inv[...], axis=0), NN)
        D[...] = A[k, at, :] - dot(left_parts(w), CR[at, :], NT)

    D[...] = A[0, :B, :]
    split_column(0)
    inv[...] = invert()
    for k in range(nb - 1):
        next_pivot(k + 1)
        eliminate(k)
        split_column(k + 1)
        inv[...] = invert()
    eliminate(nb - 1)
    end_ref[...] = jnp.zeros_like(end_ref)


def gram_inverse(me, parts, nb, pieces):
    width = nb * B
    out = jax.ShapeDtypeStruct((width, width), BF16)
    return pl.pallas_call(
        functools.partial(inverse_kernel, nb=nb, pieces=pieces),
        out_shape=(out, out, jax.ShapeDtypeStruct((8, B), F32)),
        in_specs=[pl.BlockSpec(memory_space=pltpu.SMEM)]
        + [pl.BlockSpec(memory_space=pltpu.VMEM) for _ in parts],
        out_specs=(pl.BlockSpec(memory_space=pltpu.VMEM),) * 3,
        scratch_shapes=[pltpu.VMEM((pieces * p[3], B), F32) for p in chunk_plan(nb, pieces)]
        + [
            pltpu.VMEM((nb, width, B), F32),
            pltpu.VMEM((B, B), F32),
            pltpu.VMEM((B, B), F32),
            pltpu.VMEM((B, B), F32),
            pltpu.VMEM((width, B), F32),
            pltpu.VMEM((width, 6 * B), BF16),
            pltpu.VMEM((width, 6 * B), BF16),
            pltpu.VMEM((width, 6 * B), BF16),
        ],
        compiler_params=pltpu.CompilerParams(vmem_limit_bytes=32 * MIB),
        cost_estimate=pl.CostEstimate(
            flops=24 * width**3, bytes_accessed=width * width * 8, transcendentals=0
        ),
        name="gram_inverse",
    )(me, *parts)


def score_kernel(me_ref, flag_ref, hi_ref, lo_ref, t_ref, scale_ref, end_ref, *refs, rows, masks):
    parts, out_ref, evals = refs[:-2], refs[-2], refs[-1]
    e = pl.program_id(0)

    @pl.when(e == 0)
    def _():
        for part, held in zip(parts, masks):
            for q, mask in enumerate(held):
                to = pl.multiple_of((me_ref[0] ^ mask) * rows, 16)
                evals[pl.ds(to, rows), :] = part[q * rows : (q + 1) * rows, :]

    @pl.when(flag_ref[e] > 0)
    def _():
        block = evals[pl.ds(pl.multiple_of(e * EB, EB), EB), :]
        pre = (dot(block, hi_ref[...], NN) + dot(block, lo_ref[...], NN)).astype(BF16)
        score = dot(pre, t_ref[...], NT)
        out_ref[pl.ds(e, 1), :] = jnp.max(score, axis=0, keepdims=True) * scale_ref[...]

    @pl.when(flag_ref[e] <= 0)
    def _():
        out_ref[pl.ds(e, 1), :] = jnp.zeros((1, out_ref.shape[1]), F32)


def scores(index, flags, parts, masks, rows, hi, lo, t, scale, end):
    total = sum(p.shape[0] for p in parts)
    blocks = total // EB
    width = t.shape[1]
    whole = lambda shape: pl.BlockSpec(shape, lambda e: (0, 0))
    smem = pl.BlockSpec(memory_space=pltpu.SMEM)
    operands = (hi, lo, t, scale, end) + tuple(parts)
    return pl.pallas_call(
        functools.partial(score_kernel, rows=rows, masks=masks),
        grid=(blocks,),
        out_shape=jax.ShapeDtypeStruct((blocks, t.shape[0]), F32),
        in_specs=[smem, smem] + [whole(x.shape) for x in operands],
        out_specs=whole((blocks, t.shape[0])),
        scratch_shapes=[pltpu.VMEM((total, width), BF16)],
        compiler_params=pltpu.CompilerParams(vmem_limit_bytes=20 * MIB + 8 * total * width),
        cost_estimate=pl.CostEstimate(
            flops=6 * total * width * width,
            bytes_accessed=total * width * 2 + width * width * 6,
            transcendentals=0,
        ),
        name="scores",
    )(index, flags, *operands)


def bit_groups(n):
    bits = [1 << s for s in range(n.bit_length() - 1)]
    groups = [[b] for b in bits[:2]]
    rest = bits[2:]
    while rest:
        groups.append(rest[:2])
        rest = rest[2:]
    return groups


def send(x, mask, n):
    return lax.ppermute(x, "dp", [(i, i ^ mask) for i in range(n)])


def exchange_orders(n):
    groups = bit_groups(n)
    return [groups[:1] + groups[:0:-1], groups]


def place_of(index, order, n):
    place, step = 0, n
    for group in order:
        size = 1 << len(group)
        step //= size
        place = place + (index // group[0]) % size * step
    return place


def spread_out(x, group, n):
    return [x] + [send(x, q * group[0], n) for q in range(1, 1 << len(group))]


def gather_stage(x, masks, group, n):
    steps = [q * group[0] for q in range(1 << len(group))]
    return jnp.concatenate(spread_out(x, group, n)), [m ^ step for step in steps for m in masks]


def all_reduce(chunks, evals, orders, n):
    first = orders[0][0][0]
    chunks = [keep + send(other, first, n) for keep, other in chunks]
    groups, masks = bit_groups(n), [0]
    for group in groups[1:2] + groups[3:]:
        evals, masks = gather_stage(evals, masks, group, n)
    stages = len(orders[0])
    for s in range(1, stages):
        after = []
        for x, order in zip(chunks, orders):
            size = 1 << len(order[s])
            part = x.shape[0] // size
            total = x[:part]
            for q in range(1, size):
                total = total + send(x[q * part : (q + 1) * part], q * order[s][0], n)
            after.append(total)
        chunks, evals = lax.optimization_barrier((after, evals))
    for s in range(stages - 1, 0, -1):
        chunks = [
            jnp.concatenate(spread_out(x, order[s], n)) for x, order in zip(chunks, orders)
        ]
        chunks = lax.optimization_barrier(chunks)
    return [(x, send(x, first, n)) for x in chunks], evals, masks


def per_device(train_grads, eval_grads, pair_eval, pair_count, n):
    width = train_grads.shape[1]
    nb = width // B
    index = lax.axis_index("dp")
    orders = exchange_orders(n)
    me = jnp.stack([place_of(index, order, n) for order in orders])
    halves = local_gram(me, train_grads, n)
    chunks, evals, masks = all_reduce(
        list(zip(halves[::2], halves[1::2])), eval_grads, orders, n
    )
    blocks = eval_grads.shape[0] * n // EB
    squares = jnp.sum(jnp.square(train_grads.astype(F32)), axis=1)
    scale = lax.rsqrt(squares + EPSILON)[None, :]
    order, count = pair_eval[index], pair_count[index]
    hits = order[:, None] == jnp.arange(blocks, dtype=jnp.int32)[None, :]
    inside = jnp.arange(order.shape[0], dtype=jnp.int32)[:, None] < count
    flags = jnp.any(hits & inside, axis=0).astype(jnp.int32)
    chunks, evals, scale, flags = lax.optimization_barrier((chunks, evals, scale, flags))
    groups = bit_groups(n)
    for group in groups[2:3]:
        evals, masks = gather_stage(evals, masks, group, n)
    hi, lo, end = gram_inverse(me, [x for pair in chunks for x in pair], nb, n)
    evals, end = lax.optimization_barrier((evals, end))
    parts = spread_out(evals, groups[0], n)
    masks = [masks, [m ^ groups[0][0] for m in masks]]
    return scores(
        index[None], flags, parts, masks, eval_grads.shape[0], hi, lo, train_grads, scale, end
    )


def solution(mesh):
    placed = (P(("groups", "dp"), None), P(("groups", "dp"), None), P("groups", None), P("groups"))
    return jax.shard_map(
        functools.partial(per_device, n=mesh.shape["dp"]),
        mesh=mesh,
        in_specs=placed,
        out_specs=P(None, ("groups", "dp")),
        check_vma=False,
    )
```
